32 devices in a mesh: rows: 4 (over y, core), cols: 8 (over z, x).
Axes of the slice: x: 2, y: 2, z: 4, core: 2. Of those that a mesh axis runs over, the one named last changes fastest.
Arguments:
- lot_features: bfloat16 [8192, 512], P(('rows', 'cols')), may hold values from -60 to 60
- slot_features: bfloat16 [8192, 512], P(('cols', 'rows')), may hold values from -60 to 60
- lot_mass: float32 [8192], P('rows'), may hold values from 0.5 to 2
- slot_mass: float32 [8192], P('cols'), may hold values from 0.5 to 2
Outputs:
- lot_grad: float32 [8192, 512], P(('rows', 'cols'))
The draws below stay inside these ranges and needn't reach their ends.
All inputs are finite; a program needn't handle non-finite values.
Results may differ from the reference program's by a relative error of at most 0.0034.
Values may be sent and summed in bfloat16 or wider, within the bound.
A program may use at most 64 MiB of HBM per device.

```python
import math
import jax
import jax.numpy as jnp
from jax import lax

F = 512
ITERS = 3
LOT_DEV = 2048
N = 8192
M = 8192
N_ROWS = 4


def far_rows(key, count):
    pick_key = jax.random.fold_in(key, 1)
    one_key = jax.random.fold_in(key, 2)
    chance = jax.random.uniform(pick_key, (count,), jnp.float32) < 0.1
    forced = jnp.arange(count) == jax.random.randint(one_key, (), 0, count)
    return jnp.logical_or(chance, forced)


def feature_rows(key, count, width, hidden_spread):
    values = jnp.clip(jax.random.normal(jax.random.fold_in(key, 3), (count, width), jnp.float32), -6.0, 6.0)
    far = far_rows(key, count)
    scales = jnp.exp(jax.random.uniform(jax.random.fold_in(key, 4), (count,), jnp.float32, 0.0, hidden_spread))
    factor = jnp.where(far, 10.0, scales)
    return (values * factor[:, None]).astype(jnp.bfloat16)


def draw_lot_features(key, part):
    key = jax.random.fold_in(key, 11)
    return feature_rows(key, N, F, 0.0)


def draw_slot_features(key, part):
    key = jax.random.fold_in(key, 23)
    return feature_rows(key, M, F, 0.0)


def block_levels(own_key, extent, cuts, smallest, top_value):
    level, own = 1.0, jax.random.fold_in(own_key, 6)
    for dim, shards_of in cuts:
        steps = jnp.exp(jax.random.uniform(jax.random.fold_in(own, dim), (shards_of,), jnp.float32, smallest / len(cuts), top_value / len(cuts)))
        level = level * jnp.repeat(steps, extent[dim] // shards_of).reshape([-1 if axis == dim else 1 for axis in range(len(extent))])
    return level


def setup_inputs(seed: int = 0) -> dict:
    key_list = jax.random.split(jax.random.key(seed), 5)
    lot_features = draw_lot_features(jax.random.fold_in(key_list[4], 71), 0)
    slot_features = draw_slot_features(jax.random.fold_in(key_list[4], 71), 0)
    lot_mass = jnp.clip(jnp.exp(math.log(2.0) - 1.3862944 * jax.random.uniform(key_list[2], (N,), jnp.float32) ** block_levels(key_list[2], (N,), ((0, 4),), -0.2, 0.2)), 0.5, 2.0)
    slot_mass = jnp.clip(jnp.exp(math.log(2.0) - 1.3862944 * jax.random.uniform(key_list[3], (M,), jnp.float32) ** block_levels(key_list[3], (M,), ((0, 8),), -0.2, 0.2)), 0.5, 2.0)
    return dict(lot_features=lot_features, slot_features=slot_features, lot_mass=lot_mass, slot_mass=slot_mass)


EPS = 1.0


def cost_block(lot_block, slot_features, slot_sq):
    lot_sq = jnp.sum(lot_block.astype(jnp.float32) ** 2, axis=1)
    inner = lax.dot_general(lot_block, slot_features, (((1,), (1,)), ((), ())), preferred_element_type=jnp.float32)
    return (lot_sq[:, None] + slot_sq[None, :] - 2.0 * inner) * (0.5 / (F ** 0.5))


def reference(lot_features, slot_features, lot_mass, slot_mass):
    slot_sq = jnp.sum(slot_features.astype(jnp.float32) ** 2, axis=1)
    blocks = lot_features.reshape(N_ROWS, LOT_DEV, F)
    log_lot = jnp.log(lot_mass).reshape(N_ROWS, LOT_DEV)
    log_slot = jnp.log(slot_mass)
    slot_pot = jnp.zeros((M,), jnp.float32)
    lot_pot = jnp.zeros((N_ROWS, LOT_DEV), jnp.float32)
    for step in range(ITERS):
        def lot_update(pair):
            block, logs = pair
            scores = (slot_pot[None, :] - cost_block(block, slot_features, slot_sq)) / EPS
            return EPS * logs - EPS * jax.nn.logsumexp(scores, axis=1)

        lot_pot = lax.map(lot_update, (blocks, log_lot))

        def col_part(pair):
            block, pots = pair
            scores = (pots[:, None] - cost_block(block, slot_features, slot_sq)) / EPS
            peaks = jnp.max(scores, axis=0)
            return peaks, jnp.sum(jnp.exp(scores - peaks[None, :]), axis=0)

        peaks, totals = lax.map(col_part, (blocks, lot_pot))
        top = jnp.max(peaks, axis=0)
        whole = jnp.sum(totals * jnp.exp(peaks - top[None, :]), axis=0)
        slot_pot = EPS * log_slot - EPS * (top + jnp.log(whole))

    def grad_block(pair):
        block, pots = pair
        plan = jnp.exp((pots[:, None] + slot_pot[None, :] - cost_block(block, slot_features, slot_sq)) / EPS)
        row_total = jnp.sum(plan, axis=1)
        moved = jnp.dot(plan.astype(jnp.bfloat16), slot_features, preferred_element_type=jnp.float32)
        return row_total[:, None] * block.astype(jnp.float32) - moved

    return lax.map(grad_block, (blocks, lot_pot)).reshape(N, F)
```

```python
import functools
import math

import jax
import jax.numpy as jnp
from jax import lax
from jax.experimental import pallas as pl
from jax.experimental.pallas import tpu as pltpu
from jax.sharding import PartitionSpec as P

ITERS = 3
LANES = 128
LOG2E = 1.0 / math.log(2.0)
MESH = pl.DeviceIdType.MESH


def near_first(size):
    table = []
    for here in range(size):
        others = sorted((abs(there - here), there) for there in range(size) if there != here)
        table.append([here] + [there for _, there in others])
    return table


def pick(table, here, step):
    value = jnp.int32(table[0][step])
    for index in range(1, len(table)):
        value = jnp.where(here == index, jnp.int32(table[index][step]), value)
    return value


def lse_rows(parts):
    top = functools.reduce(jnp.maximum, parts)
    total = functools.reduce(jnp.add, [jnp.exp2(part - top) for part in parts])
    return top + jnp.log2(total)


def kernel(
    n_rows, n_cols, x_ref, y_ref, lmass_ref, smass_ref, out_ref,
    x_all, y_all, tile, x_aux, y_aux, f_col, g_dense, mf, mg,
    row_parts, col_parts, plan, row_sum, sib_out, sib_in, far_out, far_in, acc,
    xh_send, xh_recv, xl_send, xl_recv, yh_send, yh_recv, yl_send, yl_recv,
    xa_send, xa_recv, ya_send, ya_recv, row_send, row_recv, col_send, col_recv,
    sib_send, sib_recv, far_send, far_recv,
):
    r = lax.axis_index("rows")
    c = lax.axis_index("cols")
    block, width = x_ref.shape
    per = block // LANES
    lots, slots = n_rows * block, n_cols * block
    lot_groups, slot_groups = lots // LANES, slots // LANES
    unit = LOG2E / width**0.5

    barrier = pltpu.get_barrier_semaphore()
    for d in range(1, n_rows):
        pl.semaphore_signal(barrier, inc=1, device_id=(lax.rem(r + d, n_rows), c), device_id_type=MESH)
    for d in range(1, n_cols):
        pl.semaphore_signal(barrier, inc=1, device_id=(r, lax.rem(c + d, n_cols)), device_id_type=MESH)
    pl.semaphore_wait(barrier, n_rows + n_cols - 2)

    pending = []

    def push(src, dst, send, recv, target, when=None):
        copy = pltpu.make_async_remote_copy(
            src_ref=src, dst_ref=dst, send_sem=send, recv_sem=recv,
            device_id=target, device_id_type=MESH,
        )
        if when is None:
            copy.start()
        else:
            pl.when(when)(copy.start)
        pending.append((copy, when))
        return copy

    def landed(dst, send, recv):
        pltpu.make_async_remote_copy(
            src_ref=dst, dst_ref=dst, send_sem=send, recv_sem=recv,
            device_id=(r, c), device_id_type=MESH,
        ).wait_recv()

    class Gather:
        def __init__(self, buf, own, hi, lo, index, target, h_send, h_recv, l_send, l_recv):
            self.buf, self.own, self.hi, self.lo = buf, own, hi, lo
            self.h, self.l = index // lo, lax.rem(index, lo)
            self.target = target
            self.sems = h_send, h_recv, l_send, l_recv
            self.table = near_first(hi)

        def place(self, h, l):
            return pl.ds(pl.multiple_of((h * self.lo + l) * block, block), block)

        def step(self, j):
            h_send, h_recv, l_send, l_recv = self.sems
            src_h = self.h if j == 0 else pick(self.table, self.h, j)
            dst = self.buf.at[self.place(src_h, self.l)]
            if j == 0:
                src = self.own
                for way in (0, 1):
                    to = self.h + (2 * way - 1)
                    ok = jnp.logical_and(to >= 0, to < self.hi)
                    push(src, dst, h_send.at[way, 0], h_recv.at[src_h], self.target(to, self.l), ok)
            else:
                src = dst
                landed(dst, h_send.at[0, j], h_recv.at[src_h])
                to = jnp.where(src_h < self.h, self.h + 1, self.h - 1)
                ok = jnp.logical_and(to >= 0, to < self.hi)
                push(src, dst, h_send.at[0, j], h_recv.at[src_h], self.target(to, self.l), ok)
            for e in range(1, self.lo):
                to = lax.rem(self.l + e, self.lo)
                push(src, dst, l_send.at[e, j], l_recv.at[self.l, src_h], self.target(self.h, to))
            return src_h * self.lo + self.l

        def cross(self, j, e):
            _, _, l_send, l_recv = self.sems
            src_h = self.h if j == 0 else pick(self.table, self.h, j)
            src_l = lax.rem(self.l + e, self.lo)
            landed(self.buf.at[self.place(src_h, src_l)], l_send.at[e, j], l_recv.at[src_l, src_h])
            return src_h * self.lo + src_l

    r_lo = 2 if n_rows % 2 == 0 else 1
    r_hi = n_rows // r_lo
    c_hi = 4 if n_cols % 4 == 0 else n_cols
    c_lo = n_cols // c_hi
    gx = Gather(x_all, x_ref, r_hi, r_lo, r, lambda h, l: (h * r_lo + l, c), xh_send, xh_recv, xl_send, xl_recv)
    gy = Gather(y_all, y_ref, c_hi, c_lo, c, lambda h, l: (r, h * c_lo + l), yh_send, yh_recv, yl_send, yl_recv)
    gx.step(0)
    gy.step(0)
    x_all[pl.ds(pl.multiple_of(r * block, block), block), :] = x_ref[...]
    y_all[pl.ds(pl.multiple_of(c * block, block), block), :] = y_ref[...]

    squares = y_ref[...].astype(jnp.float32) ** 2
    high = squares.astype(jnp.bfloat16)
    low = (squares - high.astype(jnp.float32)).astype(jnp.bfloat16)
    ones = jnp.ones((16, width), jnp.bfloat16)
    dims = (((1,), (1,)), ((), ()))
    sq = lax.dot_general(ones, high, dims, preferred_element_type=jnp.float32)
    sq = sq + lax.dot_general(ones, low, dims, preferred_element_type=jnp.float32)
    y_aux[c, 0:8, :] = sq[0:8] * (-0.5 * unit)
    y_aux[c, 8:16, :] = jnp.broadcast_to(jnp.log2(smass_ref[pl.ds(r, 1), :]), (8, block))
    x_aux[r, :, :] = jnp.broadcast_to(jnp.log2(lmass_ref[pl.ds(c, 1), :]), (8, block))
    for d in range(1, n_rows):
        push(x_aux.at[r], x_aux.at[r], xa_send.at[d], xa_recv.at[d], (lax.rem(r + d, n_rows), c))
    for d in range(1, n_cols):
        push(y_aux.at[c], y_aux.at[c], ya_send.at[d], ya_recv.at[d], (r, lax.rem(c + d, n_cols)))

    for j in range(1, r_hi):
        gx.step(j)
    for j in range(r_hi):
        for e in range(1, r_lo):
            gx.cross(j, e)

    def fill(cb):
        ys = y_all[pl.ds(pl.multiple_of(cb * block, block), block), :]

        @pl.loop(0, lots // 256)
        def _(i):
            rows = pl.ds(pl.multiple_of(i * 256, 256), 256)
            inner = lax.dot_general(x_all[rows, :], ys, dims, preferred_element_type=jnp.float32) * unit
            for t in range(per):
                tile[cb * per + t, rows, :] = inner[:, t * LANES : (t + 1) * LANES]

    fill(c)
    for j in range(1, c_hi):
        cb = gy.step(j)
        fill(cb)
        for e in range(1, c_lo):
            fill(gy.cross(j - 1, e))
    for e in range(1, c_lo):
        fill(gy.cross(c_hi - 1, e))

    for d in range(1, n_rows):
        landed(x_aux.at[lax.rem(r + n_rows - d, n_rows)], xa_send.at[d], xa_recv.at[d])
    for d in range(1, n_cols):
        landed(y_aux.at[lax.rem(c + n_cols - d, n_cols)], ya_send.at[d], ya_recv.at[d])
    for n in range(slot_groups):
        cut = slice((n % per) * LANES, (n % per + 1) * LANES)
        g_dense[n : n + 1, :] = y_aux[n // per, 0:1, cut]
        mg[n : n + 1, :] = y_aux[n // per, 8:9, cut]
    for n in range(lot_groups):
        cut = slice((n % per) * LANES, (n % per + 1) * LANES)
        mf[n : n + 1, :] = x_aux[n // per, 0:1, cut]

    for it in range(ITERS):
        @pl.loop(0, lot_groups)
        def _(b):
            pots = [g_dense[n : n + 1, :] for n in range(slot_groups)]
            pieces = []
            for q in range(LANES // 16):
                rows = pl.ds(pl.multiple_of(b * LANES + q * 16, 16), 16)
                pieces.append(lse_rows([tile[n, rows, :] + pots[n] for n in range(slot_groups)]))
            turned = jnp.concatenate(pieces, axis=0).T
            top = jnp.max(turned, axis=0, keepdims=True)
            total = jnp.sum(jnp.exp2(turned - top), axis=0, keepdims=True)
            row_parts[it, r, pl.ds(b, 1), :] = top + jnp.log2(total)

        for d in range(1, n_rows):
            here = row_parts.at[it, r]
            push(here, here, row_send.at[it, d], row_recv.at[it, d], (lax.rem(r + d, n_rows), c))
        for d in range(1, n_rows):
            landed(row_parts.at[it, lax.rem(r + n_rows - d, n_rows)], row_send.at[it, d], row_recv.at[it, d])
        f_dense = mf[...] - lse_rows([row_parts[it, k] for k in range(n_rows)])
        for n in range(lot_groups):
            f_col[n * LANES : (n + 1) * LANES, :] = jnp.broadcast_to(f_dense[n : n + 1, :], (LANES, LANES)).T

        @pl.loop(0, slot_groups)
        def _(n):
            tops, totals = [], []
            for q in range(lots // LANES):
                rows = slice(q * LANES, (q + 1) * LANES)
                score = (tile[n, rows, :] + f_col[rows, :]).reshape(LANES // 8, 8, LANES)
                top = jnp.max(score, axis=0)
                tops.append(top)
                totals.append(jnp.sum(jnp.exp2(score - top[None]), axis=0))
            top = jnp.max(functools.reduce(jnp.maximum, tops), axis=0, keepdims=True)
            total = functools.reduce(jnp.add, [s * jnp.exp2(t - top) for s, t in zip(totals, tops)])
            total = jnp.sum(total, axis=0, keepdims=True)
            col_parts[it, c, pl.ds(n, 1), :] = top + jnp.log2(total)

        for d in range(1, n_cols):
            here = col_parts.at[it, c]
            push(here, here, col_send.at[it, d], col_recv.at[it, d], (r, lax.rem(c + d, n_cols)))
        for d in range(1, n_cols):
            landed(col_parts.at[it, lax.rem(c + n_cols - d, n_cols)], col_send.at[it, d], col_recv.at[it, d])
        g_dense[...] = mg[...] - lse_rows([col_parts[it, k] for k in range(n_cols)])

    chunk = 64

    def share(lb):
        base = pl.multiple_of(lb * block, block)

        @pl.loop(0, block // chunk)
        def _(i):
            rows = pl.ds(pl.multiple_of(base + i * chunk, chunk), chunk)
            here = pl.ds(pl.multiple_of(i * chunk, chunk), chunk)
            pots = f_col[rows, :]
            total = jnp.zeros((chunk, LANES), jnp.float32)
            for n in range(slot_groups):
                part = jnp.exp2(tile[n, rows, :] + g_dense[n : n + 1, :] + pots)
                total = total + part
                plan[here, n * LANES : (n + 1) * LANES] = part.astype(jnp.bfloat16)
            row_sum[here, :] = jnp.broadcast_to(jnp.sum(total, axis=1, keepdims=True), (chunk, LANES))

        moved = jnp.dot(plan[...], y_all[...], preferred_element_type=jnp.float32)
        return row_sum[:, 0:1] * x_all[pl.ds(base, block), :].astype(jnp.float32) - moved

    h, core = r // r_lo, lax.rem(r, r_lo)
    for d in list(range(1, r_hi)) + [0]:
        to_h = lax.rem(h + d, r_hi)
        for e in range(1, r_lo):
            to_l = lax.rem(core + e, r_lo)
            sib_out[d, e] = share(to_h * r_lo + to_l).astype(jnp.bfloat16)
            push(sib_out.at[d, e], sib_in.at[d, e], sib_send.at[d, e], sib_recv.at[d, e], (h * r_lo + to_l, c))
        acc[...] = share(to_h * r_lo + core)
        for e in range(1, r_lo):
            landed(sib_in.at[d, e], sib_send.at[d, e], sib_recv.at[d, e])
            acc[...] += sib_in[d, e].astype(jnp.float32)
        if d:
            far_out[d] = acc[...].astype(jnp.bfloat16)
            push(far_out.at[d], far_in.at[d], far_send.at[d], far_recv.at[d], (to_h * r_lo + core, c))
    for d in range(1, r_hi):
        landed(far_in.at[d], far_send.at[d], far_recv.at[d])
        acc[...] += far_in[d].astype(jnp.float32)
    out_ref[...] = acc[...]

    for copy, when in pending:
        if when is None:
            copy.wait_send()
        else:
            pl.when(when)(copy.wait_send)


def local(n_rows, n_cols, lot_features, slot_features, lot_mass, slot_mass):
    block, width = lot_features.shape
    lots, slots = n_rows * block, n_cols * block
    f32, bf16 = jnp.float32, jnp.bfloat16
    r_lo = 2 if n_rows % 2 == 0 else 1
    r_hi = n_rows // r_lo
    c_hi = 4 if n_cols % 4 == 0 else n_cols
    c_lo = n_cols // c_hi
    dma = pltpu.SemaphoreType.DMA
    sems = [
        dma((2, r_hi)), dma((r_hi,)), dma((r_lo, r_hi)), dma((r_lo, r_hi)),
        dma((2, c_hi)), dma((c_hi,)), dma((c_lo, c_hi)), dma((c_lo, c_hi)),
        dma((n_rows,)), dma((n_rows,)), dma((n_cols,)), dma((n_cols,)),
        dma((ITERS, n_rows)), dma((ITERS, n_rows)), dma((ITERS, n_cols)), dma((ITERS, n_cols)),
        dma((r_hi, r_lo)), dma((r_hi, r_lo)), dma((r_hi,)), dma((r_hi,)),
    ]
    vmem = pltpu.VMEM
    return pl.pallas_call(
        functools.partial(kernel, n_rows, n_cols),
        out_shape=jax.ShapeDtypeStruct((block, width), f32),
        in_specs=[pl.BlockSpec(memory_space=vmem)] * 4,
        out_specs=pl.BlockSpec(memory_space=vmem),
        scratch_shapes=[
            vmem((lots, width), bf16),
            vmem((slots, width), bf16),
            vmem((slots // LANES, lots, LANES), f32),
            vmem((n_rows, 8, block), f32),
            vmem((n_cols, 16, block), f32),
            vmem((lots, LANES), f32),
            vmem((slots // LANES, LANES), f32),
            vmem((lots // LANES, LANES), f32),
            vmem((slots // LANES, LANES), f32),
            vmem((ITERS, n_rows, lots // LANES, LANES), f32),
            vmem((ITERS, n_cols, slots // LANES, LANES), f32),
            vmem((block, slots), bf16),
            vmem((block, LANES), f32),
            vmem((r_hi, r_lo, block, width), bf16),
            vmem((r_hi, r_lo, block, width), bf16),
            vmem((r_hi, block, width), bf16),
            vmem((r_hi, block, width), bf16),
            vmem((block, width), f32),
        ] + sems,
        compiler_params=pltpu.CompilerParams(
            collective_id=0, has_side_effects=True, vmem_limit_bytes=48 * 1024 * 1024
        ),
        cost_estimate=pl.CostEstimate(
            flops=4 * lots * slots * width,
            bytes_accessed=4 * block * width * 2,
            transcendentals=7 * lots * slots,
        ),
    )(
        lot_features, slot_features,
        lot_mass.reshape(n_cols, block), slot_mass.reshape(n_rows, block),
    )


def solution(mesh):
    placed = (P(("rows", "cols"), None), P(("cols", "rows"), None), P("rows"), P("cols"))
    return jax.shard_map(
        functools.partial(local, mesh.shape["rows"], mesh.shape["cols"]),
        mesh=mesh, in_specs=placed, out_specs=P(("rows", "cols"), None), check_vma=False,
    )
```

```python
import functools
import math

import jax
import jax.numpy as jnp
from jax import lax
from jax.experimental import pallas as pl
from jax.experimental.pallas import tpu as pltpu
from jax.sharding import PartitionSpec as P

ITERS = 3
LANES = 128
LOG2E = 1.0 / math.log(2.0)
MESH = pl.DeviceIdType.MESH


def near_first(size):
    table = []
    for here in range(size):
        others = sorted((abs(there - here), there) for there in range(size) if there != here)
        table.append([here] + [there for _, there in others])
    return table


def pick(table, here, step):
    value = jnp.int32(table[0][step])
    for index in range(1, len(table)):
        value = jnp.where(here == index, jnp.int32(table[index][step]), value)
    return value


def lse_rows(parts):
    top = functools.reduce(jnp.maximum, parts)
    total = functools.reduce(jnp.add, [jnp.exp2(part - top) for part in parts])
    return top + jnp.log2(total)


def kernel(
    n_rows, n_cols, x_ref, y_ref, lmass_ref, smass_ref, out_ref,
    x_all, y_all, tile, x_aux, y_aux, f_col, g_dense, mf, mg,
    row_parts, col_parts, plan, row_sum, sib_out, sib_in, far_out, far_in, acc,
    xh_send, xh_recv, xl_send, xl_recv, yh_send, yh_recv, yl_send, yl_recv,
    xa_send, xa_recv, ya_send, ya_recv, row_send, row_recv, col_send, col_recv,
    sib_send, sib_recv, far_send, far_recv, own_sem, peak, total_ref, col_peak, col_total,
):
    r = lax.axis_index("rows")
    c = lax.axis_index("cols")
    block, width = x_ref.shape
    per = block // LANES
    lots, slots = n_rows * block, n_cols * block
    lot_groups, slot_groups = lots // LANES, slots // LANES
    unit = LOG2E / width**0.5

    barrier = pltpu.get_barrier_semaphore()
    for d in range(1, n_rows):
        pl.semaphore_signal(barrier, inc=1, device_id=(lax.rem(r + d, n_rows), c), device_id_type=MESH)
    for d in range(1, n_cols):
        pl.semaphore_signal(barrier, inc=1, device_id=(r, lax.rem(c + d, n_cols)), device_id_type=MESH)
    pl.semaphore_wait(barrier, n_rows + n_cols - 2)

    pending = []

    def push(src, dst, send, recv, target, when=None):
        copy = pltpu.make_async_remote_copy(
            src_ref=src, dst_ref=dst, send_sem=send, recv_sem=recv,
            device_id=target, device_id_type=MESH,
        )
        if when is None:
            copy.start()
        else:
            pl.when(when)(copy.start)
        pending.append((copy, when))
        return copy

    def landed(dst, send, recv):
        pltpu.make_async_remote_copy(
            src_ref=dst, dst_ref=dst, send_sem=send, recv_sem=recv,
            device_id=(r, c), device_id_type=MESH,
        ).wait_recv()

    class Gather:
        def __init__(self, buf, own, hi, lo, index, target, h_send, h_recv, l_send, l_recv):
            self.buf, self.own, self.hi, self.lo = buf, own, hi, lo
            self.h, self.l = index // lo, lax.rem(index, lo)
            self.target = target
            self.sems = h_send, h_recv, l_send, l_recv
            self.table = near_first(hi)

        def place(self, h, l):
            return pl.ds(pl.multiple_of((h * self.lo + l) * block, block), block)

        def step(self, j):
            h_send, h_recv, l_send, l_recv = self.sems
            src_h = self.h if j == 0 else pick(self.table, self.h, j)
            dst = self.buf.at[self.place(src_h, self.l)]
            if j == 0:
                src = self.own
                for way in (0, 1):
                    to = self.h + (2 * way - 1)
                    ok = jnp.logical_and(to >= 0, to < self.hi)
                    push(src, dst, h_send.at[way, 0], h_recv.at[src_h], self.target(to, self.l), ok)
            else:
                src = dst
                landed(dst, h_send.at[0, j], h_recv.at[src_h])
                to = jnp.where(src_h < self.h, self.h + 1, self.h - 1)
                ok = jnp.logical_and(to >= 0, to < self.hi)
                push(src, dst, h_send.at[0, j], h_recv.at[src_h], self.target(to, self.l), ok)
            for e in range(1, self.lo):
                to = lax.rem(self.l + e, self.lo)
                push(src, dst, l_send.at[e, j], l_recv.at[self.l, src_h], self.target(self.h, to))
            return src_h * self.lo + self.l

        def cross(self, j, e):
            _, _, l_send, l_recv = self.sems
            src_h = self.h if j == 0 else pick(self.table, self.h, j)
            src_l = lax.rem(self.l + e, self.lo)
            landed(self.buf.at[self.place(src_h, src_l)], l_send.at[e, j], l_recv.at[src_l, src_h])
            return src_h * self.lo + src_l

    r_lo = 2 if n_rows % 2 == 0 else 1
    r_hi = n_rows // r_lo
    c_hi = 4 if n_cols % 4 == 0 else n_cols
    c_lo = n_cols // c_hi
    gx = Gather(x_all, x_ref, r_hi, r_lo, r, lambda h, l: (h * r_lo + l, c), xh_send, xh_recv, xl_send, xl_recv)
    gy = Gather(y_all, y_ref, c_hi, c_lo, c, lambda h, l: (r, h * c_lo + l), yh_send, yh_recv, yl_send, yl_recv)
    gx.step(0)
    gy.step(0)
    own_y = pl.ds(pl.multiple_of(c * block, block), block)
    own_x = pl.ds(pl.multiple_of(r * block, block), block)
    mine = [
        pltpu.make_async_copy(y_ref, y_all.at[own_y, :], own_sem.at[0]),
        pltpu.make_async_copy(x_ref, x_all.at[own_x, :], own_sem.at[1]),
    ]
    for copy in mine:
        copy.start()
    mine[0].wait()

    squares = y_all[own_y, :].astype(jnp.float32) ** 2
    high = squares.astype(jnp.bfloat16)
    low = (squares - high.astype(jnp.float32)).astype(jnp.bfloat16)
    ones = jnp.ones((16, width), jnp.bfloat16)
    dims = (((1,), (1,)), ((), ()))
    sq = lax.dot_general(ones, high, dims, preferred_element_type=jnp.float32)
    sq = sq + lax.dot_general(ones, low, dims, preferred_element_type=jnp.float32)
    y_aux[c, 0:8, :] = sq[0:8] * (-0.5 * unit)
    y_aux[c, 8:16, :] = jnp.broadcast_to(jnp.log2(smass_ref[pl.ds(r, 1), :]), (8, block))
    x_aux[r, :, :] = jnp.broadcast_to(jnp.log2(lmass_ref[pl.ds(c, 1), :]), (8, block))
    for d in range(1, n_rows):
        push(x_aux.at[r], x_aux.at[r], xa_send.at[d], xa_recv.at[d], (lax.rem(r + d, n_rows), c))
    for d in range(1, n_cols):
        push(y_aux.at[c], y_aux.at[c], ya_send.at[d], ya_recv.at[d], (r, lax.rem(c + d, n_cols)))

    mine[1].wait()
    for j in range(1, r_hi):
        gx.step(j)
    for j in range(r_hi):
        for e in range(1, r_lo):
            gx.cross(j, e)

    def fill(cb, first=False):
        ys = y_all[pl.ds(pl.multiple_of(cb * block, block), block), :]

        @pl.loop(0, lots // 256)
        def _(i):
            rows = pl.ds(pl.multiple_of(i * 256, 256), 256)
            inner = lax.dot_general(x_all[rows, :], ys, dims, preferred_element_type=jnp.float32) * unit
            parts = [inner[:, t * LANES : (t + 1) * LANES] for t in range(per)]
            for t in range(per):
                tile[cb * per + t, rows, :] = parts[t]
            scores = [parts[t] + y_aux[cb, 0:1, t * LANES : (t + 1) * LANES] for t in range(per)]
            top = functools.reduce(jnp.maximum, scores)
            if not first:
                before = peak[rows, :]
                top = jnp.maximum(top, before)
            sums = functools.reduce(jnp.add, [jnp.exp2(score - top) for score in scores])
            if not first:
                sums = sums + total_ref[rows, :] * jnp.exp2(before - top)
            peak[rows, :] = top
            total_ref[rows, :] = sums

    fill(c, True)
    for d in range(1, n_cols):
        landed(y_aux.at[lax.rem(c + n_cols - d, n_cols)], ya_send.at[d], ya_recv.at[d])
    for j in range(1, c_hi):
        cb = gy.step(j)
        fill(cb)
        for e in range(1, c_lo):
            fill(gy.cross(j - 1, e))
    for e in range(1, c_lo):
        fill(gy.cross(c_hi - 1, e))

    for d in range(1, n_rows):
        landed(x_aux.at[lax.rem(r + n_rows - d, n_rows)], xa_send.at[d], xa_recv.at[d])
    for n in range(slot_groups):
        cut = slice((n % per) * LANES, (n % per + 1) * LANES)
        mg[n : n + 1, :] = y_aux[n // per, 8:9, cut]
    for n in range(lot_groups):
        cut = slice((n % per) * LANES, (n % per + 1) * LANES)
        mf[n : n + 1, :] = x_aux[n // per, 0:1, cut]

    for it in range(ITERS):
        if it:
            @pl.loop(0, lot_groups)
            def _(b):
                pots = [g_dense[n : n + 1, :] for n in range(slot_groups)]
                for q in range(LANES // 16):
                    rows = pl.ds(pl.multiple_of(b * LANES + q * 16, 16), 16)
                    peak[rows, :] = lse_rows([tile[n, rows, :] + pots[n] for n in range(slot_groups)])

        for b in range(lot_groups):
            rows = slice(b * LANES, (b + 1) * LANES)
            turned = (peak[rows, :] if it else peak[rows, :] + jnp.log2(total_ref[rows, :])).T
            top = jnp.max(turned, axis=0, keepdims=True)
            total = jnp.sum(jnp.exp2(turned - top), axis=0, keepdims=True)
            row_parts[it, r, b : b + 1, :] = top + jnp.log2(total)

        for d in range(1, n_rows):
            here = row_parts.at[it, r]
            push(here, here, row_send.at[it, d], row_recv.at[it, d], (lax.rem(r + d, n_rows), c))
        for d in range(1, n_rows):
            landed(row_parts.at[it, lax.rem(r + n_rows - d, n_rows)], row_send.at[it, d], row_recv.at[it, d])
        f_dense = mf[...] - lse_rows([row_parts[it, k] for k in range(n_rows)])
        for n in range(lot_groups):
            f_col[n * LANES : (n + 1) * LANES, :] = jnp.broadcast_to(f_dense[n : n + 1, :], (LANES, LANES)).T

        @pl.loop(0, slot_groups)
        def _(n):
            tops, totals = [], []
            for q in range(lots // LANES):
                rows = slice(q * LANES, (q + 1) * LANES)
                score = (tile[n, rows, :] + f_col[rows, :]).reshape(LANES // 8, 8, LANES)
                top = jnp.max(score, axis=0)
                tops.append(top)
                totals.append(jnp.sum(jnp.exp2(score - top[None]), axis=0))
            top = functools.reduce(jnp.maximum, tops)
            col_peak[n] = top
            col_total[n] = functools.reduce(jnp.add, [s * jnp.exp2(t - top) for s, t in zip(totals, tops)])

        for n in range(slot_groups):
            top = jnp.max(col_peak[n], axis=0, keepdims=True)
            total = jnp.sum(col_total[n] * jnp.exp2(col_peak[n] - top), axis=0, keepdims=True)
            col_parts[it, c, n : n + 1, :] = top + jnp.log2(total)

        for d in range(1, n_cols):
            here = col_parts.at[it, c]
            push(here, here, col_send.at[it, d], col_recv.at[it, d], (r, lax.rem(c + d, n_cols)))
        for d in range(1, n_cols):
            landed(col_parts.at[it, lax.rem(c + n_cols - d, n_cols)], col_send.at[it, d], col_recv.at[it, d])
        g_dense[...] = mg[...] - lse_rows([col_parts[it, k] for k in range(n_cols)])

    chunk = 64

    def share(lb):
        base = pl.multiple_of(lb * block, block)

        @pl.loop(0, block // chunk)
        def _(i):
            rows = pl.ds(pl.multiple_of(base + i * chunk, chunk), chunk)
            here = pl.ds(pl.multiple_of(i * chunk, chunk), chunk)
            pots = f_col[rows, :]
            total = jnp.zeros((chunk, LANES), jnp.float32)
            for n in range(slot_groups):
                part = jnp.exp2(tile[n, rows, :] + g_dense[n : n + 1, :] + pots)
                total = total + part
                plan[here, n * LANES : (n + 1) * LANES] = part.astype(jnp.bfloat16)
            row_sum[here, :] = jnp.broadcast_to(jnp.sum(total, axis=1, keepdims=True), (chunk, LANES))

        moved = jnp.dot(plan[...], y_all[...], preferred_element_type=jnp.float32)
        return row_sum[:, 0:1] * x_all[pl.ds(base, block), :].astype(jnp.float32) - moved

    h, core = r // r_lo, lax.rem(r, r_lo)
    for d in list(range(1, r_hi)) + [0]:
        to_h = lax.rem(h + d, r_hi)
        for e in range(1, r_lo):
            to_l = lax.rem(core + e, r_lo)
            sib_out[d, e] = share(to_h * r_lo + to_l).astype(jnp.bfloat16)
            push(sib_out.at[d, e], sib_in.at[d, e], sib_send.at[d, e], sib_recv.at[d, e], (h * r_lo + to_l, c))
        acc[...] = share(to_h * r_lo + core)
        for e in range(1, r_lo):
            landed(sib_in.at[d, e], sib_send.at[d, e], sib_recv.at[d, e])
            acc[...] += sib_in[d, e].astype(jnp.float32)
        if d:
            far_out[d] = acc[...].astype(jnp.bfloat16)
            push(far_out.at[d], far_in.at[d], far_send.at[d], far_recv.at[d], (to_h * r_lo + core, c))
    for d in range(1, r_hi):
        landed(far_in.at[d], far_send.at[d], far_recv.at[d])
        acc[...] += far_in[d].astype(jnp.float32)
    out_ref[...] = acc[...]

    for copy, when in pending:
        if when is None:
            copy.wait_send()
        else:
            pl.when(when)(copy.wait_send)


def local(n_rows, n_cols, lot_features, slot_features, lot_mass, slot_mass):
    block, width = lot_features.shape
    lots, slots = n_rows * block, n_cols * block
    f32, bf16 = jnp.float32, jnp.bfloat16
    r_lo = 2 if n_rows % 2 == 0 else 1
    r_hi = n_rows // r_lo
    c_hi = 4 if n_cols % 4 == 0 else n_cols
    c_lo = n_cols // c_hi
    dma = pltpu.SemaphoreType.DMA
    sems = [
        dma((2, r_hi)), dma((r_hi,)), dma((r_lo, r_hi)), dma((r_lo, r_hi)),
        dma((2, c_hi)), dma((c_hi,)), dma((c_lo, c_hi)), dma((c_lo, c_hi)),
        dma((n_rows,)), dma((n_rows,)), dma((n_cols,)), dma((n_cols,)),
        dma((ITERS, n_rows)), dma((ITERS, n_rows)), dma((ITERS, n_cols)), dma((ITERS, n_cols)),
        dma((r_hi, r_lo)), dma((r_hi, r_lo)), dma((r_hi,)), dma((r_hi,)),
    ]
    vmem = pltpu.VMEM
    return pl.pallas_call(
        functools.partial(kernel, n_rows, n_cols),
        out_shape=jax.ShapeDtypeStruct((block, width), f32),
        in_specs=[pl.BlockSpec(memory_space=pl.ANY)] * 2 + [pl.BlockSpec(memory_space=vmem)] * 2,
        out_specs=pl.BlockSpec(memory_space=vmem),
        scratch_shapes=[
            vmem((lots, width), bf16),
            vmem((slots, width), bf16),
            vmem((slots // LANES, lots, LANES), f32),
            vmem((n_rows, 8, block), f32),
            vmem((n_cols, 16, block), f32),
            vmem((lots, LANES), f32),
            vmem((slots // LANES, LANES), f32),
            vmem((lots // LANES, LANES), f32),
            vmem((slots // LANES, LANES), f32),
            vmem((ITERS, n_rows, lots // LANES, LANES), f32),
            vmem((ITERS, n_cols, slots // LANES, LANES), f32),
            vmem((block, slots), bf16),
            vmem((block, LANES), f32),
            vmem((r_hi, r_lo, block, width), bf16),
            vmem((r_hi, r_lo, block, width), bf16),
            vmem((r_hi, block, width), bf16),
            vmem((r_hi, block, width), bf16),
            vmem((block, width), f32),
        ] + sems + [
            dma((2,)),
            vmem((lots, LANES), f32),
            vmem((lots, LANES), f32),
            vmem((slots // LANES, 8, LANES), f32),
            vmem((slots // LANES, 8, LANES), f32),
        ],
        compiler_params=pltpu.CompilerParams(
            collective_id=0, has_side_effects=True, vmem_limit_bytes=48 * 1024 * 1024
        ),
        cost_estimate=pl.CostEstimate(
            flops=4 * lots * slots * width,
            bytes_accessed=4 * block * width * 2,
            transcendentals=7 * lots * slots,
        ),
    )(
        lot_features, slot_features,
        lot_mass.reshape(n_cols, block), slot_mass.reshape(n_rows, block),
    )


def solution(mesh):
    placed = (P(("rows", "cols"), None), P(("cols", "rows"), None), P("rows"), P("cols"))
    return jax.shard_map(
        functools.partial(local, mesh.shape["rows"], mesh.shape["cols"]),
        mesh=mesh, in_specs=placed, out_specs=P(("rows", "cols"), None), check_vma=False,
    )
```

```python
import functools
import math

import jax
import jax.numpy as jnp
from jax import lax
from jax.experimental import pallas as pl
from jax.experimental.pallas import tpu as pltpu
from jax.sharding import PartitionSpec as P

ITERS = 3
PIECES = 2
LANES = 128
LOG2E = 1.0 / math.log(2.0)
MESH = pl.DeviceIdType.MESH


def near_first(size):
    table = []
    for here in range(size):
        others = sorted((abs(there - here), there) for there in range(size) if there != here)
        table.append([here] + [there for _, there in others])
    return table


def pick(table, here, step):
    value = jnp.int32(table[0][step])
    for index in range(1, len(table)):
        value = jnp.where(here == index, jnp.int32(table[index][step]), value)
    return value


def lse_rows(parts):
    top = functools.reduce(jnp.maximum, parts)
    total = functools.reduce(jnp.add, [jnp.exp2(part - top) for part in parts])
    return top + jnp.log2(total)


def kernel(
    n_rows, n_cols, x_ref, y_ref, lmass_ref, smass_ref, out_ref,
    x_all, y_all, tile, x_aux, y_aux, f_col, g_dense, mf, mg,
    row_parts, col_parts, plan, row_sum, sib_out, sib_in, far_out, far_in, acc,
    xh_send, xh_recv, xl_send, xl_recv, yh_send, yh_recv, yl_send, yl_recv,
    xa_send, xa_recv, ya_send, ya_recv, row_send, row_recv, col_send, col_recv,
    sib_send, sib_recv, far_send, far_recv, own_sem, peak, total_ref, col_peak, col_total, mass,
):
    r = lax.axis_index("rows")
    c = lax.axis_index("cols")
    block, width = x_ref.shape
    per = block // LANES
    lots, slots = n_rows * block, n_cols * block
    lot_groups, slot_groups = lots // LANES, slots // LANES
    unit = LOG2E / width**0.5

    barrier = pltpu.get_barrier_semaphore()
    for d in range(1, n_rows):
        pl.semaphore_signal(barrier, inc=1, device_id=(lax.rem(r + d, n_rows), c), device_id_type=MESH)
    for d in range(1, n_cols):
        pl.semaphore_signal(barrier, inc=1, device_id=(r, lax.rem(c + d, n_cols)), device_id_type=MESH)
    pl.semaphore_wait(barrier, n_rows + n_cols - 2)

    pending = []

    def push(src, dst, send, recv, target, when=None):
        copy = pltpu.make_async_remote_copy(
            src_ref=src, dst_ref=dst, send_sem=send, recv_sem=recv,
            device_id=target, device_id_type=MESH,
        )
        if when is None:
            copy.start()
        else:
            pl.when(when)(copy.start)
        pending.append((copy, when))
        return copy

    def landed(dst, send, recv):
        pltpu.make_async_remote_copy(
            src_ref=dst, dst_ref=dst, send_sem=send, recv_sem=recv,
            device_id=(r, c), device_id_type=MESH,
        ).wait_recv()

    class Gather:
        def __init__(self, buf, own, hi, lo, index, target, h_send, h_recv, l_send, l_recv):
            self.buf, self.own, self.hi, self.lo = buf, own, hi, lo
            self.h, self.l = index // lo, lax.rem(index, lo)
            self.target = target
            self.sems = h_send, h_recv, l_send, l_recv
            self.table = near_first(hi)

        def place(self, h, l, p):
            rows = block // PIECES
            return pl.ds(pl.multiple_of((h * self.lo + l) * block + p * rows, rows), rows)

        def source(self, j):
            return self.h if j == 0 else pick(self.table, self.h, j)

        def number(self, j, e=0):
            return self.source(j) * self.lo + lax.rem(self.l + e, self.lo)

        def step(self, j, p):
            h_send, h_recv, l_send, l_recv = self.sems
            src_h = self.source(j)
            dst = self.buf.at[self.place(src_h, self.l, p)]
            if j == 0:
                src = self.own.at[pl.ds(p * (block // PIECES), block // PIECES)]
                for way in (0, 1):
                    to = self.h + (2 * way - 1)
                    ok = jnp.logical_and(to >= 0, to < self.hi)
                    push(src, dst, h_send.at[way, 0, p], h_recv.at[src_h, p], self.target(to, self.l), ok)
            else:
                src = dst
                landed(dst, h_send.at[0, j, p], h_recv.at[src_h, p])
                to = jnp.where(src_h < self.h, self.h + 1, self.h - 1)
                ok = jnp.logical_and(to >= 0, to < self.hi)
                push(src, dst, h_send.at[0, j, p], h_recv.at[src_h, p], self.target(to, self.l), ok)
            for e in range(1, self.lo):
                to = lax.rem(self.l + e, self.lo)
                push(src, dst, l_send.at[e, j, p], l_recv.at[self.l, src_h, p], self.target(self.h, to))

        def cross(self, j, e):
            _, _, l_send, l_recv = self.sems
            src_h = self.source(j)
            src_l = lax.rem(self.l + e, self.lo)
            for p in range(PIECES):
                landed(self.buf.at[self.place(src_h, src_l, p)], l_send.at[e, j, p], l_recv.at[src_l, src_h, p])

    r_lo = 2 if n_rows % 2 == 0 else 1
    r_hi = n_rows // r_lo
    c_hi = 4 if n_cols % 4 == 0 else n_cols
    c_lo = n_cols // c_hi
    gx = Gather(x_all, x_ref, r_hi, r_lo, r, lambda h, l: (h * r_lo + l, c), xh_send, xh_recv, xl_send, xl_recv)
    gy = Gather(y_all, y_ref, c_hi, c_lo, c, lambda h, l: (r, h * c_lo + l), yh_send, yh_recv, yl_send, yl_recv)
    for p in range(PIECES):
        gy.step(0, p)
        gx.step(0, p)
    own_y = pl.ds(pl.multiple_of(c * block, block), block)
    own_x = pl.ds(pl.multiple_of(r * block, block), block)
    mine = [
        pltpu.make_async_copy(y_ref, y_all.at[own_y, :], own_sem.at[0]),
        pltpu.make_async_copy(x_ref, x_all.at[own_x, :], own_sem.at[1]),
    ]
    for copy in mine:
        copy.start()
    masses = [
        pltpu.make_async_copy(lmass_ref.at[own_y], mass.at[0], own_sem.at[2]),
        pltpu.make_async_copy(smass_ref.at[own_x], mass.at[1], own_sem.at[3]),
    ]
    for copy in masses:
        copy.start()
    for copy in masses:
        copy.wait()
    mine[0].wait()

    squares = y_all[own_y, :].astype(jnp.float32) ** 2
    high = squares.astype(jnp.bfloat16)
    low = (squares - high.astype(jnp.float32)).astype(jnp.bfloat16)
    ones = jnp.ones((16, width), jnp.bfloat16)
    dims = (((1,), (1,)), ((), ()))
    sq = lax.dot_general(ones, high, dims, preferred_element_type=jnp.float32)
    sq = sq + lax.dot_general(ones, low, dims, preferred_element_type=jnp.float32)
    y_aux[c, 0:8, :] = sq[0:8] * (-0.5 * unit)
    y_aux[c, 8:16, :] = jnp.broadcast_to(jnp.log2(mass[1:2, :]), (8, block))
    x_aux[r, :, :] = jnp.broadcast_to(jnp.log2(mass[0:1, :]), (8, block))
    for d in range(1, n_rows):
        push(x_aux.at[r], x_aux.at[r], xa_send.at[d], xa_recv.at[d], (lax.rem(r + d, n_rows), c))
    for d in range(1, n_cols):
        push(y_aux.at[c], y_aux.at[c], ya_send.at[d], ya_recv.at[d], (r, lax.rem(c + d, n_cols)))

    mine[1].wait()
    early = min(3, c_hi)
    gy.step(1, 0)
    for j in range(1, r_hi):
        for p in range(PIECES):
            gx.step(j, p)
    for p in range(PIECES):
        for j in range(1, early):
            if p or j > 1:
                gy.step(j, p)
    for j in range(r_hi):
        for e in range(1, r_lo):
            gx.cross(j, e)

    def fill(cb, first=False):
        ys = y_all[pl.ds(pl.multiple_of(cb * block, block), block), :]

        @pl.loop(0, lots // 256)
        def _(i):
            rows = pl.ds(pl.multiple_of(i * 256, 256), 256)
            inner = lax.dot_general(x_all[rows, :], ys, dims, preferred_element_type=jnp.float32) * unit
            parts = [inner[:, t * LANES : (t + 1) * LANES] for t in range(per)]
            for t in range(per):
                tile[cb * per + t, rows, :] = parts[t]
            scores = [parts[t] + y_aux[cb, 0:1, t * LANES : (t + 1) * LANES] for t in range(per)]
            top = functools.reduce(jnp.maximum, scores)
            if not first:
                before = peak[rows, :]
                top = jnp.maximum(top, before)
            sums = functools.reduce(jnp.add, [jnp.exp2(score - top) for score in scores])
            if not first:
                sums = sums + total_ref[rows, :] * jnp.exp2(before - top)
            peak[rows, :] = top
            total_ref[rows, :] = sums

    fill(c, True)
    for d in range(1, n_cols):
        landed(y_aux.at[lax.rem(c + n_cols - d, n_cols)], ya_send.at[d], ya_recv.at[d])
    def fill_crossed(j):
        for e in range(1, c_lo):
            gy.cross(j, e)
            fill(gy.number(j, e))

    fill_crossed(0)
    late = [(j, p) for j in range(early, c_hi) for p in range(PIECES)]
    for j in range(1, early):
        if late:
            gy.step(*late.pop(0))
        fill(gy.number(j))
    for j, p in late:
        gy.step(j, p)
    fill_crossed(1)
    for j in range(early, c_hi):
        fill(gy.number(j))
    for j in range(2, c_hi):
        fill_crossed(j)

    for d in range(1, n_rows):
        landed(x_aux.at[lax.rem(r + n_rows - d, n_rows)], xa_send.at[d], xa_recv.at[d])
    for n in range(slot_groups):
        cut = slice((n % per) * LANES, (n % per + 1) * LANES)
        mg[n : n + 1, :] = y_aux[n // per, 8:9, cut]
    for n in range(lot_groups):
        cut = slice((n % per) * LANES, (n % per + 1) * LANES)
        mf[n : n + 1, :] = x_aux[n // per, 0:1, cut]

    for it in range(ITERS):
        if it:
            @pl.loop(0, lot_groups)
            def _(b):
                pots = [g_dense[n : n + 1, :] for n in range(slot_groups)]
                for q in range(LANES // 16):
                    rows = pl.ds(pl.multiple_of(b * LANES + q * 16, 16), 16)
                    peak[rows, :] = lse_rows([tile[n, rows, :] + pots[n] for n in range(slot_groups)])

        for b in range(lot_groups):
            rows = slice(b * LANES, (b + 1) * LANES)
            turned = (peak[rows, :] if it else peak[rows, :] + jnp.log2(total_ref[rows, :])).T
            top = jnp.max(turned, axis=0, keepdims=True)
            total = jnp.sum(jnp.exp2(turned - top), axis=0, keepdims=True)
            row_parts[it, r, b : b + 1, :] = top + jnp.log2(total)

        for d in range(1, n_rows):
            here = row_parts.at[it, r]
            push(here, here, row_send.at[it, d], row_recv.at[it, d], (lax.rem(r + d, n_rows), c))
        for d in range(1, n_rows):
            landed(row_parts.at[it, lax.rem(r + n_rows - d, n_rows)], row_send.at[it, d], row_recv.at[it, d])
        f_dense = mf[...] - lse_rows([row_parts[it, k] for k in range(n_rows)])
        for n in range(lot_groups):
            f_col[n * LANES : (n + 1) * LANES, :] = jnp.broadcast_to(f_dense[n : n + 1, :], (LANES, LANES)).T

        @pl.loop(0, slot_groups)
        def _(n):
            tops, totals = [], []
            for q in range(lots // LANES):
                rows = slice(q * LANES, (q + 1) * LANES)
                score = (tile[n, rows, :] + f_col[rows, :]).reshape(LANES // 8, 8, LANES)
                top = jnp.max(score, axis=0)
                tops.append(top)
                totals.append(jnp.sum(jnp.exp2(score - top[None]), axis=0))
            top = functools.reduce(jnp.maximum, tops)
            col_peak[n] = top
            col_total[n] = functools.reduce(jnp.add, [s * jnp.exp2(t - top) for s, t in zip(totals, tops)])

        for n in range(slot_groups):
            top = jnp.max(col_peak[n], axis=0, keepdims=True)
            total = jnp.sum(col_total[n] * jnp.exp2(col_peak[n] - top), axis=0, keepdims=True)
            col_parts[it, c, n : n + 1, :] = top + jnp.log2(total)

        for d in range(1, n_cols):
            here = col_parts.at[it, c]
            push(here, here, col_send.at[it, d], col_recv.at[it, d], (r, lax.rem(c + d, n_cols)))
        for d in range(1, n_cols):
            landed(col_parts.at[it, lax.rem(c + n_cols - d, n_cols)], col_send.at[it, d], col_recv.at[it, d])
        g_dense[...] = mg[...] - lse_rows([col_parts[it, k] for k in range(n_cols)])

    chunk = 64

    def share(lb, start, count):
        base = pl.multiple_of(lb * block + start, count)

        @pl.loop(0, count // chunk)
        def _(i):
            rows = pl.ds(pl.multiple_of(base + i * chunk, chunk), chunk)
            here = pl.ds(pl.multiple_of(i * chunk, chunk), chunk)
            pots = f_col[rows, :]
            total = jnp.zeros((chunk, LANES), jnp.float32)
            for n in range(slot_groups):
                part = jnp.exp2(tile[n, rows, :] + g_dense[n : n + 1, :] + pots)
                total = total + part
                plan[here, n * LANES : (n + 1) * LANES] = part.astype(jnp.bfloat16)
            row_sum[here, :] = jnp.broadcast_to(jnp.sum(total, axis=1, keepdims=True), (chunk, LANES))

        moved = jnp.dot(plan[0:count, :], y_all[...], preferred_element_type=jnp.float32)
        return row_sum[0:count, 0:1] * x_all[pl.ds(base, count), :].astype(jnp.float32) - moved

    h, core = r // r_lo, lax.rem(r, r_lo)
    half = block // PIECES
    for d in list(range(1, r_hi)) + [0]:
        to_h = lax.rem(h + d, r_hi)
        cuts = [(p, p * half, half) for p in range(PIECES)] if d else [(0, 0, block)]
        for p, start, count in cuts:
            cut = slice(start, start + count)
            for e in range(1, r_lo):
                to_l = lax.rem(core + e, r_lo)
                sib_out[d, e, cut, :] = share(to_h * r_lo + to_l, start, count).astype(jnp.bfloat16)
                push(
                    sib_out.at[d, e, cut], sib_in.at[d, e, cut], sib_send.at[d, e, p], sib_recv.at[d, e, p],
                    (h * r_lo + to_l, c),
                )
            part = share(to_h * r_lo + core, start, count)
            for e in range(1, r_lo):
                landed(sib_in.at[d, e, cut], sib_send.at[d, e, p], sib_recv.at[d, e, p])
                part = part + sib_in[d, e, cut, :].astype(jnp.float32)
            if d:
                far_out[d, cut, :] = part.astype(jnp.bfloat16)
                push(
                    far_out.at[d, cut], far_in.at[d, cut], far_send.at[d, p], far_recv.at[d, p],
                    (to_h * r_lo + core, c),
                )
            else:
                acc[...] = part
    for d in range(1, r_hi):
        for p in range(PIECES):
            cut = slice(p * half, (p + 1) * half)
            landed(far_in.at[d, cut], far_send.at[d, p], far_recv.at[d, p])
            acc[cut, :] += far_in[d, cut, :].astype(jnp.float32)
    out_ref[...] = acc[...]

    for copy, when in pending:
        if when is None:
            copy.wait_send()
        else:
            pl.when(when)(copy.wait_send)


def local(n_rows, n_cols, lot_features, slot_features, lot_mass, slot_mass):
    block, width = lot_features.shape
    lots, slots = n_rows * block, n_cols * block
    f32, bf16 = jnp.float32, jnp.bfloat16
    r_lo = 2 if n_rows % 2 == 0 else 1
    r_hi = n_rows // r_lo
    c_hi = 4 if n_cols % 4 == 0 else n_cols
    c_lo = n_cols // c_hi
    dma = pltpu.SemaphoreType.DMA
    sems = [
        dma((2, r_hi, PIECES)), dma((r_hi, PIECES)), dma((r_lo, r_hi, PIECES)), dma((r_lo, r_hi, PIECES)),
        dma((2, c_hi, PIECES)), dma((c_hi, PIECES)), dma((c_lo, c_hi, PIECES)), dma((c_lo, c_hi, PIECES)),
        dma((n_rows,)), dma((n_rows,)), dma((n_cols,)), dma((n_cols,)),
        dma((ITERS, n_rows)), dma((ITERS, n_rows)), dma((ITERS, n_cols)), dma((ITERS, n_cols)),
        dma((r_hi, r_lo, PIECES)), dma((r_hi, r_lo, PIECES)), dma((r_hi, PIECES)), dma((r_hi, PIECES)),
    ]
    vmem = pltpu.VMEM
    return pl.pallas_call(
        functools.partial(kernel, n_rows, n_cols),
        out_shape=jax.ShapeDtypeStruct((block, width), f32),
        in_specs=[pl.BlockSpec(memory_space=pl.ANY)] * 4,
        out_specs=pl.BlockSpec(memory_space=vmem),
        scratch_shapes=[
            vmem((lots, width), bf16),
            vmem((slots, width), bf16),
            vmem((slots // LANES, lots, LANES), f32),
            vmem((n_rows, 8, block), f32),
            vmem((n_cols, 16, block), f32),
            vmem((lots, LANES), f32),
            vmem((slots // LANES, LANES), f32),
            vmem((lots // LANES, LANES), f32),
            vmem((slots // LANES, LANES), f32),
            vmem((ITERS, n_rows, lots // LANES, LANES), f32),
            vmem((ITERS, n_cols, slots // LANES, LANES), f32),
            vmem((block, slots), bf16),
            vmem((block, LANES), f32),
            vmem((r_hi, r_lo, block, width), bf16),
            vmem((r_hi, r_lo, block, width), bf16),
            vmem((r_hi, block, width), bf16),
            vmem((r_hi, block, width), bf16),
            vmem((block, width), f32),
        ] + sems + [
            dma((4,)),
            vmem((lots, LANES), f32),
            vmem((lots, LANES), f32),
            vmem((slots // LANES, 8, LANES), f32),
            vmem((slots // LANES, 8, LANES), f32),
            vmem((2, block), f32),
        ],
        compiler_params=pltpu.CompilerParams(
            collective_id=0, has_side_effects=True, vmem_limit_bytes=62 * 1024 * 1024
        ),
        cost_estimate=pl.CostEstimate(
            flops=4 * lots * slots * width,
            bytes_accessed=4 * block * width * 2,
            transcendentals=7 * lots * slots,
        ),
    )(
        lot_features, slot_features,
        lot_mass, slot_mass,
    )


def solution(mesh):
    placed = (P(("rows", "cols"), None), P(("cols", "rows"), None), P("rows"), P("cols"))
    return jax.shard_map(
        functools.partial(local, mesh.shape["rows"], mesh.shape["cols"]),
        mesh=mesh, in_specs=placed, out_specs=P(("rows", "cols"), None), check_vma=False,
    )
```

```python
import functools
import math

import jax
import jax.numpy as jnp
from jax import lax
from jax.experimental import pallas as pl
from jax.experimental.pallas import tpu as pltpu
from jax.sharding import PartitionSpec as P

ITERS = 3
PIECES = 2
LANES = 128
LOG2E = 1.0 / math.log(2.0)
MESH = pl.DeviceIdType.MESH


def near_first(size):
    table = []
    for here in range(size):
        others = sorted((abs(there - here), there) for there in range(size) if there != here)
        table.append([here] + [there for _, there in others])
    return table


def pick(table, here, step):
    value = jnp.int32(table[0][step])
    for index in range(1, len(table)):
        value = jnp.where(here == index, jnp.int32(table[index][step]), value)
    return value


def lse_rows(parts):
    top = functools.reduce(jnp.maximum, parts)
    total = functools.reduce(jnp.add, [jnp.exp2(part - top) for part in parts])
    return top + jnp.log2(total)


def kernel(
    n_rows, n_cols, x_ref, y_ref, lmass_ref, smass_ref, out_ref,
    x_all, y_all, tile, x_aux, y_aux, f_col, g_dense, mf, mg,
    row_parts, col_parts, plan, row_sum, sib_out, sib_in, far_out, far_in, acc,
    xh_send, xh_recv, xl_send, xl_recv, yh_send, yh_recv, yl_send, yl_recv,
    xa_send, xa_recv, ya_send, ya_recv, row_send, row_recv, col_send, col_recv,
    sib_send, sib_recv, far_send, far_recv, own_sem, peak, total_ref, col_peak, col_total, mass,
):
    r = lax.axis_index("rows")
    c = lax.axis_index("cols")
    block, width = x_ref.shape
    per = block // LANES
    lots, slots = n_rows * block, n_cols * block
    lot_groups, slot_groups = lots // LANES, slots // LANES
    unit = LOG2E / width**0.5

    barrier = pltpu.get_barrier_semaphore()
    for d in range(1, n_rows):
        pl.semaphore_signal(barrier, inc=1, device_id=(lax.rem(r + d, n_rows), c), device_id_type=MESH)
    for d in range(1, n_cols):
        pl.semaphore_signal(barrier, inc=1, device_id=(r, lax.rem(c + d, n_cols)), device_id_type=MESH)
    pl.semaphore_wait(barrier, n_rows + n_cols - 2)

    pending = []

    def push(src, dst, send, recv, target, when=None):
        copy = pltpu.make_async_remote_copy(
            src_ref=src, dst_ref=dst, send_sem=send, recv_sem=recv,
            device_id=target, device_id_type=MESH,
        )
        if when is None:
            copy.start()
        else:
            pl.when(when)(copy.start)
        pending.append((copy, when))
        return copy

    def landed(dst, send, recv):
        pltpu.make_async_remote_copy(
            src_ref=dst, dst_ref=dst, send_sem=send, recv_sem=recv,
            device_id=(r, c), device_id_type=MESH,
        ).wait_recv()

    class Gather:
        def __init__(self, buf, own, hi, lo, index, target, h_send, h_recv, l_send, l_recv):
            self.buf, self.own, self.hi, self.lo = buf, own, hi, lo
            self.h, self.l = index // lo, lax.rem(index, lo)
            self.target = target
            self.sems = h_send, h_recv, l_send, l_recv
            self.table = near_first(hi)

        def place(self, h, l, p):
            rows = block // PIECES
            return pl.ds(pl.multiple_of((h * self.lo + l) * block + p * rows, rows), rows)

        def source(self, j):
            return self.h if j == 0 else pick(self.table, self.h, j)

        def number(self, j, e=0):
            return self.source(j) * self.lo + lax.rem(self.l + e, self.lo)

        def step(self, j, p):
            h_send, h_recv, l_send, l_recv = self.sems
            src_h = self.source(j)
            dst = self.buf.at[self.place(src_h, self.l, p)]
            if j == 0:
                src = self.own.at[pl.ds(p * (block // PIECES), block // PIECES)]
                for way in (0, 1):
                    to = self.h + (2 * way - 1)
                    ok = jnp.logical_and(to >= 0, to < self.hi)
                    push(src, dst, h_send.at[way, 0, p], h_recv.at[src_h, p], self.target(to, self.l), ok)
            else:
                src = dst
                landed(dst, h_send.at[0, j, p], h_recv.at[src_h, p])
                to = jnp.where(src_h < self.h, self.h + 1, self.h - 1)
                ok = jnp.logical_and(to >= 0, to < self.hi)
                push(src, dst, h_send.at[0, j, p], h_recv.at[src_h, p], self.target(to, self.l), ok)
            for e in range(1, self.lo):
                to = lax.rem(self.l + e, self.lo)
                push(src, dst, l_send.at[e, j, p], l_recv.at[self.l, src_h, p], self.target(self.h, to))

        def cross(self, j, e):
            _, _, l_send, l_recv = self.sems
            src_h = self.source(j)
            src_l = lax.rem(self.l + e, self.lo)
            for p in range(PIECES):
                landed(self.buf.at[self.place(src_h, src_l, p)], l_send.at[e, j, p], l_recv.at[src_l, src_h, p])

    r_lo = 2 if n_rows % 2 == 0 else 1
    r_hi = n_rows // r_lo
    c_hi = 4 if n_cols % 4 == 0 else n_cols
    c_lo = n_cols // c_hi
    gx = Gather(x_all, x_ref, r_hi, r_lo, r, lambda h, l: (h * r_lo + l, c), xh_send, xh_recv, xl_send, xl_recv)
    gy = Gather(y_all, y_ref, c_hi, c_lo, c, lambda h, l: (r, h * c_lo + l), yh_send, yh_recv, yl_send, yl_recv)
    for p in range(PIECES):
        gy.step(0, p)
        gx.step(0, p)
    own_y = pl.ds(pl.multiple_of(c * block, block), block)
    own_x = pl.ds(pl.multiple_of(r * block, block), block)
    mine = [
        pltpu.make_async_copy(y_ref, y_all.at[own_y, :], own_sem.at[0]),
        pltpu.make_async_copy(x_ref, x_all.at[own_x, :], own_sem.at[1]),
    ]
    for copy in mine:
        copy.start()
    masses = [
        pltpu.make_async_copy(lmass_ref.at[own_y], mass.at[0], own_sem.at[2]),
        pltpu.make_async_copy(smass_ref.at[own_x], mass.at[1], own_sem.at[3]),
    ]
    for copy in masses:
        copy.start()
    for copy in masses:
        copy.wait()
    mine[0].wait()

    squares = y_all[own_y, :].astype(jnp.float32) ** 2
    high = squares.astype(jnp.bfloat16)
    low = (squares - high.astype(jnp.float32)).astype(jnp.bfloat16)
    ones = jnp.ones((16, width), jnp.bfloat16)
    dims = (((1,), (1,)), ((), ()))
    sq = lax.dot_general(ones, high, dims, preferred_element_type=jnp.float32)
    sq = sq + lax.dot_general(ones, low, dims, preferred_element_type=jnp.float32)
    y_aux[c, 0:8, :] = sq[0:8] * (-0.5 * unit)
    y_aux[c, 8:16, :] = jnp.broadcast_to(jnp.log2(mass[1:2, :]), (8, block))
    x_aux[r, :, :] = jnp.broadcast_to(jnp.log2(mass[0:1, :]), (8, block))
    for d in range(1, n_rows):
        push(x_aux.at[r], x_aux.at[r], xa_send.at[d], xa_recv.at[d], (lax.rem(r + d, n_rows), c))
    for d in range(1, n_cols):
        push(y_aux.at[c], y_aux.at[c], ya_send.at[d], ya_recv.at[d], (r, lax.rem(c + d, n_cols)))

    mine[1].wait()
    early = min(3, c_hi)
    gy.step(1, 0)
    for j in range(1, r_hi):
        for p in range(PIECES):
            gx.step(j, p)
    for p in range(PIECES):
        for j in range(1, early):
            if p or j > 1:
                gy.step(j, p)
    for j in range(r_hi):
        for e in range(1, r_lo):
            gx.cross(j, e)

    def fill(cb, first=False):
        ys = y_all[pl.ds(pl.multiple_of(cb * block, block), block), :]

        @pl.loop(0, lots // 256)
        def _(i):
            rows = pl.ds(pl.multiple_of(i * 256, 256), 256)
            inner = lax.dot_general(x_all[rows, :], ys, dims, preferred_element_type=jnp.float32) * unit
            parts = [inner[:, t * LANES : (t + 1) * LANES] for t in range(per)]
            for t in range(per):
                tile[cb * per + t, rows, :] = parts[t]
            scores = [parts[t] + y_aux[cb, 0:1, t * LANES : (t + 1) * LANES] for t in range(per)]
            top = functools.reduce(jnp.maximum, scores)
            if not first:
                before = peak[rows, :]
                top = jnp.maximum(top, before)
            sums = functools.reduce(jnp.add, [jnp.exp2(score - top) for score in scores])
            if not first:
                sums = sums + total_ref[rows, :] * jnp.exp2(before - top)
            peak[rows, :] = top
            total_ref[rows, :] = sums

    fill(c, True)
    for d in range(1, n_cols):
        landed(y_aux.at[lax.rem(c + n_cols - d, n_cols)], ya_send.at[d], ya_recv.at[d])
    def fill_crossed(j):
        for e in range(1, c_lo):
            gy.cross(j, e)
            fill(gy.number(j, e))

    fill_crossed(0)
    late = [(j, p) for j in range(early, c_hi) for p in range(PIECES)]
    for j in range(1, early):
        if late:
            gy.step(*late.pop(0))
        fill(gy.number(j))
    for j, p in late:
        gy.step(j, p)
    fill_crossed(1)
    for j in range(early, c_hi):
        fill(gy.number(j))
    for j in range(2, c_hi):
        fill_crossed(j)

    for d in range(1, n_rows):
        landed(x_aux.at[lax.rem(r + n_rows - d, n_rows)], xa_send.at[d], xa_recv.at[d])
    for n in range(slot_groups):
        cut = slice((n % per) * LANES, (n % per + 1) * LANES)
        mg[n : n + 1, :] = y_aux[n // per, 8:9, cut]
    for n in range(lot_groups):
        cut = slice((n % per) * LANES, (n % per + 1) * LANES)
        mf[n : n + 1, :] = x_aux[n // per, 0:1, cut]

    lot_half, slot_half = lot_groups // 2, slot_groups // 2

    def send_rows(it, half):
        for d in range(1, n_rows):
            here = row_parts.at[it, half, r]
            push(here, here, row_send.at[it, half, d], row_recv.at[it, half, d], (lax.rem(r + d, n_rows), c))

    def take_rows(it, half):
        for d in range(1, n_rows):
            there = row_parts.at[it, half, lax.rem(r + n_rows - d, n_rows)]
            landed(there, row_send.at[it, half, d], row_recv.at[it, half, d])
        first = half * lot_half
        logs = mf[first : first + lot_half, :]
        f_dense = logs - lse_rows([row_parts[it, half, k] for k in range(n_rows)])
        for n in range(lot_half):
            rows = slice((first + n) * LANES, (first + n + 1) * LANES)
            f_col[rows, :] = jnp.broadcast_to(f_dense[n : n + 1, :], (LANES, LANES)).T

    def send_cols(it, half):
        for d in range(1, n_cols):
            here = col_parts.at[it, half, c]
            push(here, here, col_send.at[it, half, d], col_recv.at[it, half, d], (r, lax.rem(c + d, n_cols)))

    def take_cols(it, half):
        for d in range(1, n_cols):
            there = col_parts.at[it, half, lax.rem(c + n_cols - d, n_cols)]
            landed(there, col_send.at[it, half, d], col_recv.at[it, half, d])
        groups = slice(half * slot_half, (half + 1) * slot_half)
        g_dense[groups, :] = mg[groups, :] - lse_rows([col_parts[it, half, k] for k in range(n_cols)])

    def row_scores(half, rows, pots):
        return [tile[half * slot_half + n, rows, :] + pots[n] for n in range(slot_half)]

    def row_pots(half):
        return [g_dense[half * slot_half + n : half * slot_half + n + 1, :] for n in range(slot_half)]

    def row_first():
        @pl.loop(0, lot_groups)
        def _(b):
            pots = row_pots(0)
            for q in range(LANES // 16):
                rows = pl.ds(pl.multiple_of(b * LANES + q * 16, 16), 16)
                scores = row_scores(0, rows, pots)
                top = functools.reduce(jnp.maximum, scores)
                peak[rows, :] = top
                total_ref[rows, :] = functools.reduce(jnp.add, [jnp.exp2(score - top) for score in scores])

    def row_second(half):
        @pl.loop(half * lot_half, (half + 1) * lot_half)
        def _(b):
            pots = row_pots(1)
            for q in range(LANES // 16):
                rows = pl.ds(pl.multiple_of(b * LANES + q * 16, 16), 16)
                scores = row_scores(1, rows, pots)
                before = peak[rows, :]
                top = jnp.maximum(functools.reduce(jnp.maximum, scores), before)
                sums = functools.reduce(jnp.add, [jnp.exp2(score - top) for score in scores])
                peak[rows, :] = top
                total_ref[rows, :] = sums + total_ref[rows, :] * jnp.exp2(before - top)

    def row_close(it, half):
        for b in range(lot_half):
            rows = slice((half * lot_half + b) * LANES, (half * lot_half + b + 1) * LANES)
            turned = (peak[rows, :] + jnp.log2(total_ref[rows, :])).T
            top = jnp.max(turned, axis=0, keepdims=True)
            total = jnp.sum(jnp.exp2(turned - top), axis=0, keepdims=True)
            row_parts[it, half, r, b : b + 1, :] = top + jnp.log2(total)

    def col_scan(n, half):
        tops, totals = [], []
        span = lots // 2
        for q in range(span // LANES):
            rows = slice(half * span + q * LANES, half * span + (q + 1) * LANES)
            score = (tile[n, rows, :] + f_col[rows, :]).reshape(LANES // 8, 8, LANES)
            top = jnp.max(score, axis=0)
            tops.append(top)
            totals.append(jnp.sum(jnp.exp2(score - top[None]), axis=0))
        if half:
            tops.append(col_peak[n])
            totals.append(col_total[n])
        top = functools.reduce(jnp.maximum, tops)
        col_peak[n] = top
        col_total[n] = functools.reduce(jnp.add, [s * jnp.exp2(t - top) for s, t in zip(totals, tops)])

    def col_close(it, half):
        for n in range(slot_half):
            top8 = col_peak[half * slot_half + n]
            top = jnp.max(top8, axis=0, keepdims=True)
            total = jnp.sum(col_total[half * slot_half + n] * jnp.exp2(top8 - top), axis=0, keepdims=True)
            col_parts[it, half, c, n : n + 1, :] = top + jnp.log2(total)

    for it in range(ITERS):
        if it:
            take_cols(it - 1, 0)
            row_first()
            take_cols(it - 1, 1)
        for half in (0, 1):
            if it:
                row_second(half)
            row_close(it, half)
            send_rows(it, half)

        take_rows(it, 0)

        @pl.loop(0, slot_groups, unroll=4)
        def _(n):
            col_scan(n, 0)

        take_rows(it, 1)
        for half in (0, 1):
            @pl.loop(half * slot_half, (half + 1) * slot_half, unroll=4)
            def _(n):
                col_scan(n, 1)

            col_close(it, half)
            send_cols(it, half)
    for half in (0, 1):
        take_cols(ITERS - 1, half)

    chunk = 64

    def share(lb, start, count):
        base = pl.multiple_of(lb * block + start, count)

        @pl.loop(0, count // chunk)
        def _(i):
            rows = pl.ds(pl.multiple_of(base + i * chunk, chunk), chunk)
            here = pl.ds(pl.multiple_of(i * chunk, chunk), chunk)
            pots = f_col[rows, :]
            total = jnp.zeros((chunk, LANES), jnp.float32)
            for n in range(slot_groups):
                part = jnp.exp2(tile[n, rows, :] + g_dense[n : n + 1, :] + pots)
                total = total + part
                plan[here, n * LANES : (n + 1) * LANES] = part.astype(jnp.bfloat16)
            row_sum[here, :] = jnp.broadcast_to(jnp.sum(total, axis=1, keepdims=True), (chunk, LANES))

        moved = jnp.dot(plan[0:count, :], y_all[...], preferred_element_type=jnp.float32)
        return row_sum[0:count, 0:1] * x_all[pl.ds(base, count), :].astype(jnp.float32) - moved

    h, core = r // r_lo, lax.rem(r, r_lo)
    half = block // PIECES
    for d in list(range(1, r_hi)) + [0]:
        to_h = lax.rem(h + d, r_hi)
        cuts = [(p, p * half, half) for p in range(PIECES)] if d else [(0, 0, block)]
        for p, start, count in cuts:
            cut = slice(start, start + count)
            for e in range(1, r_lo):
                to_l = lax.rem(core + e, r_lo)
                sib_out[d, e, cut, :] = share(to_h * r_lo + to_l, start, count).astype(jnp.bfloat16)
                push(
                    sib_out.at[d, e, cut], sib_in.at[d, e, cut], sib_send.at[d, e, p], sib_recv.at[d, e, p],
                    (h * r_lo + to_l, c),
                )
            part = share(to_h * r_lo + core, start, count)
            for e in range(1, r_lo):
                landed(sib_in.at[d, e, cut], sib_send.at[d, e, p], sib_recv.at[d, e, p])
                part = part + sib_in[d, e, cut, :].astype(jnp.float32)
            if d:
                far_out[d, cut, :] = part.astype(jnp.bfloat16)
                push(
                    far_out.at[d, cut], far_in.at[d, cut], far_send.at[d, p], far_recv.at[d, p],
                    (to_h * r_lo + core, c),
                )
            else:
                acc[...] = part
    for d in range(1, r_hi):
        for p in range(PIECES):
            cut = slice(p * half, (p + 1) * half)
            landed(far_in.at[d, cut], far_send.at[d, p], far_recv.at[d, p])
            acc[cut, :] += far_in[d, cut, :].astype(jnp.float32)
    out_ref[...] = acc[...]

    for copy, when in pending:
        if when is None:
            copy.wait_send()
        else:
            pl.when(when)(copy.wait_send)


def local(n_rows, n_cols, lot_features, slot_features, lot_mass, slot_mass):
    block, width = lot_features.shape
    lots, slots = n_rows * block, n_cols * block
    f32, bf16 = jnp.float32, jnp.bfloat16
    r_lo = 2 if n_rows % 2 == 0 else 1
    r_hi = n_rows // r_lo
    c_hi = 4 if n_cols % 4 == 0 else n_cols
    c_lo = n_cols // c_hi
    dma = pltpu.SemaphoreType.DMA
    sems = [
        dma((2, r_hi, PIECES)), dma((r_hi, PIECES)), dma((r_lo, r_hi, PIECES)), dma((r_lo, r_hi, PIECES)),
        dma((2, c_hi, PIECES)), dma((c_hi, PIECES)), dma((c_lo, c_hi, PIECES)), dma((c_lo, c_hi, PIECES)),
        dma((n_rows,)), dma((n_rows,)), dma((n_cols,)), dma((n_cols,)),
        dma((ITERS, 2, n_rows)), dma((ITERS, 2, n_rows)), dma((ITERS, 2, n_cols)), dma((ITERS, 2, n_cols)),
        dma((r_hi, r_lo, PIECES)), dma((r_hi, r_lo, PIECES)), dma((r_hi, PIECES)), dma((r_hi, PIECES)),
    ]
    vmem = pltpu.VMEM
    return pl.pallas_call(
        functools.partial(kernel, n_rows, n_cols),
        out_shape=jax.ShapeDtypeStruct((block, width), f32),
        in_specs=[pl.BlockSpec(memory_space=pltpu.HBM)] * 4,
        out_specs=pl.BlockSpec(memory_space=vmem),
        scratch_shapes=[
            vmem((lots, width), bf16),
            vmem((slots, width), bf16),
            vmem((slots // LANES, lots, LANES), f32),
            vmem((n_rows, 8, block), f32),
            vmem((n_cols, 16, block), f32),
            vmem((lots, LANES), f32),
            vmem((slots // LANES, LANES), f32),
            vmem((lots // LANES, LANES), f32),
            vmem((slots // LANES, LANES), f32),
            vmem((ITERS, 2, n_rows, lots // LANES // 2, LANES), f32),
            vmem((ITERS, 2, n_cols, slots // LANES // 2, LANES), f32),
            vmem((block, slots), bf16),
            vmem((block, LANES), f32),
            vmem((r_hi, r_lo, block, width), bf16),
            vmem((r_hi, r_lo, block, width), bf16),
            vmem((r_hi, block, width), bf16),
            vmem((r_hi, block, width), bf16),
            vmem((block, width), f32),
        ] + sems + [
            dma((4,)),
            vmem((lots, LANES), f32),
            vmem((lots, LANES), f32),
            vmem((slots // LANES, 8, LANES), f32),
            vmem((slots // LANES, 8, LANES), f32),
            vmem((2, block), f32),
        ],
        compiler_params=pltpu.CompilerParams(
            collective_id=0, has_side_effects=True, vmem_limit_bytes=62 * 1024 * 1024
        ),
        cost_estimate=pl.CostEstimate(
            flops=4 * lots * slots * width,
            bytes_accessed=4 * block * width * 2,
            transcendentals=7 * lots * slots,
        ),
    )(
        lot_features, slot_features,
        lot_mass, slot_mass,
    )


def solution(mesh):
    placed = (P(("rows", "cols"), None), P(("cols", "rows"), None), P("rows"), P("cols"))
    return jax.shard_map(
        functools.partial(local, mesh.shape["rows"], mesh.shape["cols"]),
        mesh=mesh, in_specs=placed, out_specs=P(("rows", "cols"), None), check_vma=False,
    )
```

```python
import functools
import math

import jax
import jax.numpy as jnp
from jax import lax
from jax.experimental import pallas as pl
from jax.experimental.pallas import tpu as pltpu
from jax.sharding import PartitionSpec as P

ITERS = 3
PIECES = 2
LANES = 128
LOG2E = 1.0 / math.log(2.0)
MESH = pl.DeviceIdType.MESH


def near_first(size):
    table = []
    for here in range(size):
        others = sorted((abs(there - here), there) for there in range(size) if there != here)
        table.append([here] + [there for _, there in others])
    return table


def pick(table, here, step):
    value = jnp.int32(table[0][step])
    for index in range(1, len(table)):
        value = jnp.where(here == index, jnp.int32(table[index][step]), value)
    return value


def lse_rows(parts):
    top = functools.reduce(jnp.maximum, parts)
    total = functools.reduce(jnp.add, [jnp.exp2(part - top) for part in parts])
    return top + jnp.log2(total)


def kernel(
    n_rows, n_cols, x_ref, y_ref, lmass_ref, smass_ref, out_ref,
    x_all, y_all, tile, x_aux, y_aux, f_col, g_dense, mf, mg,
    row_parts, col_parts, plan, row_sum, sib_out, sib_in, far_out, far_in, acc,
    xh_send, xh_recv, xl_send, xl_recv, yh_send, yh_recv, yl_send, yl_recv,
    xa_send, xa_recv, ya_send, ya_recv, row_send, row_recv, col_send, col_recv,
    sib_send, sib_recv, far_send, far_recv, own_sem, peak, total_ref, col_peak, col_total, mass,
):
    r = lax.axis_index("rows")
    c = lax.axis_index("cols")
    block, width = x_ref.shape
    per = block // LANES
    lots, slots = n_rows * block, n_cols * block
    lot_groups, slot_groups = lots // LANES, slots // LANES
    unit = LOG2E / width**0.5

    barrier = pltpu.get_barrier_semaphore()
    for d in range(1, n_rows):
        pl.semaphore_signal(barrier, inc=1, device_id=(lax.rem(r + d, n_rows), c), device_id_type=MESH)
    for d in range(1, n_cols):
        pl.semaphore_signal(barrier, inc=1, device_id=(r, lax.rem(c + d, n_cols)), device_id_type=MESH)
    pl.semaphore_wait(barrier, n_rows + n_cols - 2)

    pending = []

    def push(src, dst, send, recv, target, when=None):
        copy = pltpu.make_async_remote_copy(
            src_ref=src, dst_ref=dst, send_sem=send, recv_sem=recv,
            device_id=target, device_id_type=MESH,
        )
        if when is None:
            copy.start()
        else:
            pl.when(when)(copy.start)
        pending.append((copy, when))
        return copy

    def landed(dst, send, recv):
        pltpu.make_async_remote_copy(
            src_ref=dst, dst_ref=dst, send_sem=send, recv_sem=recv,
            device_id=(r, c), device_id_type=MESH,
        ).wait_recv()

    class Gather:
        def __init__(self, buf, own, hi, lo, index, target, h_send, h_recv, l_send, l_recv):
            self.buf, self.own, self.hi, self.lo = buf, own, hi, lo
            self.h, self.l = index // lo, lax.rem(index, lo)
            self.target = target
            self.sems = h_send, h_recv, l_send, l_recv
            self.table = near_first(hi)

        def place(self, h, l, p):
            rows = block // PIECES
            return pl.ds(pl.multiple_of((h * self.lo + l) * block + p * rows, rows), rows)

        def source(self, j):
            return self.h if j == 0 else pick(self.table, self.h, j)

        def number(self, j, e=0):
            return self.source(j) * self.lo + lax.rem(self.l + e, self.lo)

        def step(self, j, p):
            h_send, h_recv, l_send, l_recv = self.sems
            src_h = self.source(j)
            dst = self.buf.at[self.place(src_h, self.l, p)]
            if j == 0:
                src = self.own.at[pl.ds(p * (block // PIECES), block // PIECES)]
                for way in (0, 1):
                    to = self.h + (2 * way - 1)
                    ok = jnp.logical_and(to >= 0, to < self.hi)
                    push(src, dst, h_send.at[way, 0, p], h_recv.at[src_h, p], self.target(to, self.l), ok)
            else:
                src = dst
                landed(dst, h_send.at[0, j, p], h_recv.at[src_h, p])
                to = jnp.where(src_h < self.h, self.h + 1, self.h - 1)
                ok = jnp.logical_and(to >= 0, to < self.hi)
                push(src, dst, h_send.at[0, j, p], h_recv.at[src_h, p], self.target(to, self.l), ok)
            for e in range(1, self.lo):
                to = lax.rem(self.l + e, self.lo)
                push(src, dst, l_send.at[e, j, p], l_recv.at[self.l, src_h, p], self.target(self.h, to))

        def cross(self, j, e):
            _, _, l_send, l_recv = self.sems
            src_h = self.source(j)
            src_l = lax.rem(self.l + e, self.lo)
            for p in range(PIECES):
                landed(self.buf.at[self.place(src_h, src_l, p)], l_send.at[e, j, p], l_recv.at[src_l, src_h, p])

    r_lo = 2 if n_rows % 2 == 0 else 1
    r_hi = n_rows // r_lo
    c_hi = 4 if n_cols % 4 == 0 else n_cols
    c_lo = n_cols // c_hi
    gx = Gather(x_all, x_ref, r_hi, r_lo, r, lambda h, l: (h * r_lo + l, c), xh_send, xh_recv, xl_send, xl_recv)
    gy = Gather(y_all, y_ref, c_hi, c_lo, c, lambda h, l: (r, h * c_lo + l), yh_send, yh_recv, yl_send, yl_recv)
    for p in range(PIECES):
        gy.step(0, p)
        gx.step(0, p)
    own_y = pl.ds(pl.multiple_of(c * block, block), block)
    own_x = pl.ds(pl.multiple_of(r * block, block), block)
    mine = [
        pltpu.make_async_copy(y_ref, y_all.at[own_y, :], own_sem.at[0]),
        pltpu.make_async_copy(x_ref, x_all.at[own_x, :], own_sem.at[1]),
    ]
    for copy in mine:
        copy.start()
    masses = [
        pltpu.make_async_copy(lmass_ref.at[own_y], mass.at[0], own_sem.at[2]),
        pltpu.make_async_copy(smass_ref.at[own_x], mass.at[1], own_sem.at[3]),
    ]
    for copy in masses:
        copy.start()
    for copy in masses:
        copy.wait()
    mine[0].wait()

    squares = y_all[own_y, :].astype(jnp.float32) ** 2
    high = squares.astype(jnp.bfloat16)
    low = (squares - high.astype(jnp.float32)).astype(jnp.bfloat16)
    ones = jnp.ones((16, width), jnp.bfloat16)
    dims = (((1,), (1,)), ((), ()))
    sq = lax.dot_general(ones, high, dims, preferred_element_type=jnp.float32)
    sq = sq + lax.dot_general(ones, low, dims, preferred_element_type=jnp.float32)
    y_aux[c, 0:8, :] = sq[0:8] * (-0.5 * unit)
    y_aux[c, 8:16, :] = jnp.broadcast_to(jnp.log2(mass[1:2, :]), (8, block))
    x_aux[r, :, :] = jnp.broadcast_to(jnp.log2(mass[0:1, :]), (8, block))
    for d in range(1, n_rows):
        push(x_aux.at[r], x_aux.at[r], xa_send.at[d], xa_recv.at[d], (lax.rem(r + d, n_rows), c))
    for d in range(1, n_cols):
        push(y_aux.at[c], y_aux.at[c], ya_send.at[d], ya_recv.at[d], (r, lax.rem(c + d, n_cols)))

    mine[1].wait()
    early = min(3, c_hi)
    gy.step(1, 0)
    for j in range(1, r_hi):
        for p in range(PIECES):
            gx.step(j, p)
    for p in range(PIECES):
        for j in range(1, early):
            if p or j > 1:
                gy.step(j, p)
    for j in range(r_hi):
        for e in range(1, r_lo):
            gx.cross(j, e)

    def fill(cb, first=False):
        ys = y_all[pl.ds(pl.multiple_of(cb * block, block), block), :]

        @pl.loop(0, lots // 256)
        def _(i):
            rows = pl.ds(pl.multiple_of(i * 256, 256), 256)
            inner = lax.dot_general(x_all[rows, :], ys, dims, preferred_element_type=jnp.float32) * unit
            parts = [inner[:, t * LANES : (t + 1) * LANES] for t in range(per)]
            for t in range(per):
                tile[cb * per + t, rows, :] = parts[t]
            scores = [parts[t] + y_aux[cb, 0:1, t * LANES : (t + 1) * LANES] for t in range(per)]
            top = functools.reduce(jnp.maximum, scores)
            if not first:
                before = peak[rows, :]
                top = jnp.maximum(top, before)
            sums = functools.reduce(jnp.add, [jnp.exp2(score - top) for score in scores])
            if not first:
                sums = sums + total_ref[rows, :] * jnp.exp2(before - top)
            peak[rows, :] = top
            total_ref[rows, :] = sums

    fill(c, True)
    for d in range(1, n_cols):
        landed(y_aux.at[lax.rem(c + n_cols - d, n_cols)], ya_send.at[d], ya_recv.at[d])
    def fill_crossed(j):
        for e in range(1, c_lo):
            gy.cross(j, e)
            fill(gy.number(j, e))

    fill_crossed(0)
    late = [(j, p) for j in range(early, c_hi) for p in range(PIECES)]
    for j in range(1, early):
        if late:
            gy.step(*late.pop(0))
        fill(gy.number(j))
    for j, p in late:
        gy.step(j, p)
    fill_crossed(1)
    for j in range(early, c_hi):
        fill(gy.number(j))
    for j in range(2, c_hi):
        fill_crossed(j)

    for d in range(1, n_rows):
        landed(x_aux.at[lax.rem(r + n_rows - d, n_rows)], xa_send.at[d], xa_recv.at[d])
    for n in range(slot_groups):
        cut = slice((n % per) * LANES, (n % per + 1) * LANES)
        mg[n : n + 1, :] = y_aux[n // per, 8:9, cut]
    for n in range(lot_groups):
        cut = slice((n % per) * LANES, (n % per + 1) * LANES)
        mf[n : n + 1, :] = x_aux[n // per, 0:1, cut]

    lot_half, slot_half = lot_groups // 2, slot_groups // 2

    def send_rows(it, half):
        for d in range(1, n_rows):
            here = row_parts.at[it, half, r]
            push(here, here, row_send.at[it, half, d], row_recv.at[it, half, d], (lax.rem(r + d, n_rows), c))

    def take_rows(it, half):
        for d in range(1, n_rows):
            there = row_parts.at[it, half, lax.rem(r + n_rows - d, n_rows)]
            landed(there, row_send.at[it, half, d], row_recv.at[it, half, d])
        first = half * lot_half
        logs = mf[first : first + lot_half, :]
        f_dense = logs - lse_rows([row_parts[it, half, k] for k in range(n_rows)])
        for n in range(lot_half):
            rows = slice((first + n) * LANES, (first + n + 1) * LANES)
            f_col[rows, :] = jnp.broadcast_to(f_dense[n : n + 1, :], (LANES, LANES)).T

    def send_cols(it, half):
        for d in range(1, n_cols):
            here = col_parts.at[it, half, c]
            push(here, here, col_send.at[it, half, d], col_recv.at[it, half, d], (r, lax.rem(c + d, n_cols)))

    def take_cols(it, half):
        for d in range(1, n_cols):
            there = col_parts.at[it, half, lax.rem(c + n_cols - d, n_cols)]
            landed(there, col_send.at[it, half, d], col_recv.at[it, half, d])
        groups = slice(half * slot_half, (half + 1) * slot_half)
        g_dense[groups, :] = mg[groups, :] - lse_rows([col_parts[it, half, k] for k in range(n_cols)])

    def row_scores(half, rows, pots):
        return [tile[half * slot_half + n, rows, :] + pots[n] for n in range(slot_half)]

    def row_pots(half):
        return [g_dense[half * slot_half + n : half * slot_half + n + 1, :] for n in range(slot_half)]

    def row_first():
        @pl.loop(0, lot_groups, unroll=2)
        def _(b):
            pots = row_pots(0)
            for q in range(LANES // 16):
                rows = pl.ds(pl.multiple_of(b * LANES + q * 16, 16), 16)
                scores = row_scores(0, rows, pots)
                top = functools.reduce(jnp.maximum, scores)
                peak[rows, :] = top
                total_ref[rows, :] = functools.reduce(jnp.add, [jnp.exp2(score - top) for score in scores])

    def row_second(half):
        @pl.loop(half * lot_half, (half + 1) * lot_half, unroll=2)
        def _(b):
            pots = row_pots(1)
            for q in range(LANES // 16):
                rows = pl.ds(pl.multiple_of(b * LANES + q * 16, 16), 16)
                scores = row_scores(1, rows, pots)
                before = peak[rows, :]
                top = jnp.maximum(functools.reduce(jnp.maximum, scores), before)
                sums = functools.reduce(jnp.add, [jnp.exp2(score - top) for score in scores])
                peak[rows, :] = top
                total_ref[rows, :] = sums + total_ref[rows, :] * jnp.exp2(before - top)

    def row_close(it, half):
        for b in range(lot_half):
            rows = slice((half * lot_half + b) * LANES, (half * lot_half + b + 1) * LANES)
            turned = (peak[rows, :] + jnp.log2(total_ref[rows, :])).T
            top = jnp.max(turned, axis=0, keepdims=True)
            total = jnp.sum(jnp.exp2(turned - top), axis=0, keepdims=True)
            row_parts[it, half, r, b : b + 1, :] = top + jnp.log2(total)

    def col_scan(n, half):
        tops, totals = [], []
        span = lots // 2
        for q in range(span // LANES):
            rows = slice(half * span + q * LANES, half * span + (q + 1) * LANES)
            score = (tile[n, rows, :] + f_col[rows, :]).reshape(LANES // 8, 8, LANES)
            top = jnp.max(score, axis=0)
            tops.append(top)
            totals.append(jnp.sum(jnp.exp2(score - top[None]), axis=0))
        if half:
            tops.append(col_peak[n])
            totals.append(col_total[n])
        top = functools.reduce(jnp.maximum, tops)
        col_peak[n] = top
        col_total[n] = functools.reduce(jnp.add, [s * jnp.exp2(t - top) for s, t in zip(totals, tops)])

    def col_close(it, half):
        for n in range(slot_half):
            top8 = col_peak[half * slot_half + n]
            top = jnp.max(top8, axis=0, keepdims=True)
            total = jnp.sum(col_total[half * slot_half + n] * jnp.exp2(top8 - top), axis=0, keepdims=True)
            col_parts[it, half, c, n : n + 1, :] = top + jnp.log2(total)

    for it in range(ITERS):
        if it:
            take_cols(it - 1, 0)
            row_first()
            take_cols(it - 1, 1)
        for half in (0, 1):
            if it:
                row_second(half)
            row_close(it, half)
            send_rows(it, half)

        take_rows(it, 0)

        @pl.loop(0, slot_groups, unroll=4)
        def _(n):
            col_scan(n, 0)

        take_rows(it, 1)
        for half in (0, 1):
            @pl.loop(half * slot_half, (half + 1) * slot_half, unroll=4)
            def _(n):
                col_scan(n, 1)

            col_close(it, half)
            send_cols(it, half)
    for half in (0, 1):
        take_cols(ITERS - 1, half)

    chunk = 64

    def share(lb, start, count, turn):
        base = pl.multiple_of(lb * block + start, count)

        for i in range(count // chunk):
            rows = pl.ds(pl.multiple_of(base + i * chunk, chunk), chunk)
            here = slice(i * chunk, (i + 1) * chunk)
            pots = f_col[rows, :]
            total = jnp.zeros((chunk, LANES), jnp.float32)
            for n in range(slot_groups):
                part = jnp.exp2(tile[n, rows, :] + g_dense[n : n + 1, :] + pots)
                total = total + part
                plan[turn, here, n * LANES : (n + 1) * LANES] = part.astype(jnp.bfloat16)
            row_sum[turn, here, :] = jnp.broadcast_to(jnp.sum(total, axis=1, keepdims=True), (chunk, LANES))

        moved = jnp.dot(plan[turn, 0:count, :], y_all[...], preferred_element_type=jnp.float32)
        return row_sum[turn, 0:count, 0:1] * x_all[pl.ds(base, count), :].astype(jnp.float32) - moved

    h, core = r // r_lo, lax.rem(r, r_lo)
    half = block // PIECES
    for d in list(range(1, r_hi)) + [0]:
        to_h = lax.rem(h + d, r_hi)
        cuts = [(p, p * half, half) for p in range(PIECES)] if d else [(0, 0, block)]
        for p, start, count in cuts:
            cut = slice(start, start + count)
            for e in range(1, r_lo):
                to_l = lax.rem(core + e, r_lo)
                sib_out[d, e, cut, :] = share(to_h * r_lo + to_l, start, count, 0).astype(jnp.bfloat16)
                push(
                    sib_out.at[d, e, cut], sib_in.at[d, e, cut], sib_send.at[d, e, p], sib_recv.at[d, e, p],
                    (h * r_lo + to_l, c),
                )
            part = share(to_h * r_lo + core, start, count, 1)
            for e in range(1, r_lo):
                landed(sib_in.at[d, e, cut], sib_send.at[d, e, p], sib_recv.at[d, e, p])
                part = part + sib_in[d, e, cut, :].astype(jnp.float32)
            if d:
                far_out[d, cut, :] = part.astype(jnp.bfloat16)
                push(
                    far_out.at[d, cut], far_in.at[d, cut], far_send.at[d, p], far_recv.at[d, p],
                    (to_h * r_lo + core, c),
                )
            else:
                acc[...] = part
    for p in range(PIECES):
        cut = slice(p * half, (p + 1) * half)
        result = acc[cut, :]
        for d in range(1, r_hi):
            landed(far_in.at[d, cut], far_send.at[d, p], far_recv.at[d, p])
            result = result + far_in[d, cut, :].astype(jnp.float32)
        out_ref[cut, :] = result

    for copy, when in pending:
        if when is None:
            copy.wait_send()
        else:
            pl.when(when)(copy.wait_send)


def local(n_rows, n_cols, lot_features, slot_features, lot_mass, slot_mass):
    block, width = lot_features.shape
    lots, slots = n_rows * block, n_cols * block
    f32, bf16 = jnp.float32, jnp.bfloat16
    r_lo = 2 if n_rows % 2 == 0 else 1
    r_hi = n_rows // r_lo
    c_hi = 4 if n_cols % 4 == 0 else n_cols
    c_lo = n_cols // c_hi
    dma = pltpu.SemaphoreType.DMA
    sems = [
        dma((2, r_hi, PIECES)), dma((r_hi, PIECES)), dma((r_lo, r_hi, PIECES)), dma((r_lo, r_hi, PIECES)),
        dma((2, c_hi, PIECES)), dma((c_hi, PIECES)), dma((c_lo, c_hi, PIECES)), dma((c_lo, c_hi, PIECES)),
        dma((n_rows,)), dma((n_rows,)), dma((n_cols,)), dma((n_cols,)),
        dma((ITERS, 2, n_rows)), dma((ITERS, 2, n_rows)), dma((ITERS, 2, n_cols)), dma((ITERS, 2, n_cols)),
        dma((r_hi, r_lo, PIECES)), dma((r_hi, r_lo, PIECES)), dma((r_hi, PIECES)), dma((r_hi, PIECES)),
    ]
    vmem = pltpu.VMEM
    return pl.pallas_call(
        functools.partial(kernel, n_rows, n_cols),
        out_shape=jax.ShapeDtypeStruct((block, width), f32),
        in_specs=[pl.BlockSpec(memory_space=pltpu.HBM)] * 4,
        out_specs=pl.BlockSpec(memory_space=vmem),
        scratch_shapes=[
            vmem((lots, width), bf16),
            vmem((slots, width), bf16),
            vmem((slots // LANES, lots, LANES), f32),
            vmem((n_rows, 8, block), f32),
            vmem((n_cols, 16, block), f32),
            vmem((lots, LANES), f32),
            vmem((slots // LANES, LANES), f32),
            vmem((lots // LANES, LANES), f32),
            vmem((slots // LANES, LANES), f32),
            vmem((ITERS, 2, n_rows, lots // LANES // 2, LANES), f32),
            vmem((ITERS, 2, n_cols, slots // LANES // 2, LANES), f32),
            vmem((2, block, slots), bf16),
            vmem((2, block, LANES), f32),
            vmem((r_hi, r_lo, block, width), bf16),
            vmem((r_hi, r_lo, block, width), bf16),
            vmem((r_hi, block, width), bf16),
            vmem((r_hi, block, width), bf16),
            vmem((block, width), f32),
        ] + sems + [
            dma((4,)),
            vmem((lots, LANES), f32),
            vmem((lots, LANES), f32),
            vmem((slots // LANES, 8, LANES), f32),
            vmem((slots // LANES, 8, LANES), f32),
            vmem((2, block), f32),
        ],
        compiler_params=pltpu.CompilerParams(
            collective_id=0, has_side_effects=True, vmem_limit_bytes=62 * 1024 * 1024
        ),
        cost_estimate=pl.CostEstimate(
            flops=4 * lots * slots * width,
            bytes_accessed=4 * block * width * 2,
            transcendentals=7 * lots * slots,
        ),
    )(
        lot_features, slot_features,
        lot_mass, slot_mass,
    )


def solution(mesh):
    placed = (P(("rows", "cols"), None), P(("cols", "rows"), None), P("rows"), P("cols"))
    return jax.shard_map(
        functools.partial(local, mesh.shape["rows"], mesh.shape["cols"]),
        mesh=mesh, in_specs=placed, out_specs=P(("rows", "cols"), None), check_vma=False,
    )
```
